256 devices in a mesh: cell: 32 (over x, z), wall: 8 (over y, core).
Axes of the slice: x: 4, y: 4, z: 8, core: 2. Of those that a mesh axis runs over, the one named last changes fastest.
Arguments:
- self_matrix: bfloat16 [64, 8, 1152, 1152], P('cell', 'wall'), may hold values from -0.1875 to 0.1875
- cell_source: float32 [64, 8, 3, 384], P('cell', 'wall'), may hold values from -6 to 6
- cell_pos: float32 [64, 8, 3, 384], P('cell', 'wall'), may hold values from -68 to 772, as said below
- wall_source: float32 [3, 1024, 6144], P(None, 'cell', 'wall'), may hold values from -6 to 6
- wall_coef: float32 [1024, 6144], P('cell', 'wall'), may hold values from 0.3 to 1.5
- pair_target: int32 [8, 256], P('wall'), may hold values from 0 to 63, as said below
- pair_source: int32 [8, 256], P('wall'), may hold values from 0 to 63, as said below
- pair_count: int32 [8, 32], P('wall'), may hold values from 1 to 8, as said below
- near_wall: int32 [64, 8, 1024], P('cell', 'wall'), may hold values from 0 to 51199, as said below
Outputs:
- cell_density: float32 [64, 8, 3, 384], P('cell', 'wall')
- wall_density: float32 [3, 1024, 6144], P(None, 'cell', 'wall')
The draws below stay inside these ranges and needn't reach their ends.
Inputs may be any that keep to these rules, and one draw needn't show every extreme that they name: `cell_pos`: positions of the cells' points: each cell lies about one unit inside the wall above its owner's patch. `near_wall`: each cell's list is the 32 x 2 * 16 block of its device's patch with band (rows of 800 panels) around the cell's place over the wall, in row order. `pair_target`: every slot of device o names a cell of device o. `pair_source`: every slot's source cell lies on one of the two devices next to its owner along the cell axis, around the loop. `pair_count`: in every wall index one device has all 8 slots live.
All inputs are finite; a program needn't handle non-finite values.
Results may differ from the reference program's by a relative error of at most 0.00034.
Values sent between devices are 32-bit elements; how exact they have to be, the bound alone decides.
A program may use at most 128 MiB of HBM per device.

```python
import math
import jax
import jax.numpy as jnp
from jax import lax

PTS = 384
CELL_DEV = 2
PAN_TH = 32
PAN_AX = 768
REACH = 16
PAIR_CAP = 8
NEAR_PAN = 1024
SEG = 64
NTH = 1024
NAX = 6144
EXT_AX = 800
N_CELL = 32
N_WALL = 8


panel_step = 0.125


inset_depth = 1.0


def footprints(key):
    base_key = jax.random.fold_in(key, 101)
    key_one, key_two, key_three = jax.random.split(base_key, 3)
    half_cells = CELL_DEV // 2
    edge_band = max(REACH // 4, 1)
    jitter_span = REACH // 2
    cell_ids = jnp.arange(SEG, dtype=jnp.int32)
    owner_dev = cell_ids // CELL_DEV
    local_cell = cell_ids % CELL_DEV
    lower_side = local_cell < half_cells
    junction_dev = jnp.where(lower_side, (owner_dev - 1 + N_CELL) % N_CELL, owner_dev)
    junction = junction_dev * half_cells + jnp.where(lower_side, local_cell, local_cell - half_cells)
    centres = jax.random.randint(key_one, (N_CELL * half_cells, N_WALL), jitter_span, PAN_AX - jitter_span)
    axial_off = centres[junction] + jax.random.randint(key_two, (SEG, N_WALL), -jitter_span, jitter_span + 1)
    edge_off = jax.random.randint(key_three, (SEG, N_WALL), 0, edge_band)
    theta_off = jnp.where(lower_side[:, None], edge_off, PAN_TH - edge_band + edge_off)
    return (theta_off.astype(jnp.int32), axial_off.astype(jnp.int32))


def draw_cell_pos(key, part):
    theta_off, axial_off = footprints(key)
    key = jax.random.fold_in(key, 3)
    owner_dev = jnp.arange(SEG, dtype=jnp.int32)[:, None] // CELL_DEV
    wall_row = jnp.arange(N_WALL, dtype=jnp.int32)[None, :]
    theta_idx = (owner_dev * PAN_TH + theta_off).astype(jnp.float32)
    axial_idx = (wall_row * PAN_AX + axial_off).astype(jnp.float32)
    radius = NTH * panel_step / (2.0 * math.pi) - inset_depth
    angle_rad = 2.0 * math.pi / NTH * theta_idx
    centre = jnp.stack([radius * jnp.cos(angle_rad), radius * jnp.sin(angle_rad), panel_step * axial_idx], axis=2)
    offsets = 0.5 * jax.random.normal(key, (SEG, N_WALL, 3, PTS), jnp.float32)
    return centre[:, :, :, None] + offsets


def draw_near_wall(key, part):
    theta_off, axial_off = footprints(key)
    row_index = theta_off[:, :, None, None] + jnp.arange(2 * REACH, dtype=jnp.int32)[:, None]
    col_index = axial_off[:, :, None, None] + jnp.arange(2 * REACH, dtype=jnp.int32)[None, :]
    return (row_index * EXT_AX + col_index).reshape(SEG, N_WALL, NEAR_PAN).astype(jnp.int32)


def draw_pair_count(key, part):
    key = jax.random.fold_in(key, 7)
    key_one, key_two = jax.random.split(key)
    base_count = jax.random.randint(key_one, (N_WALL, N_CELL), 1, PAIR_CAP // 2 + 1)
    busy_dev = jax.random.randint(key_two, (N_WALL, 1), 0, N_CELL)
    column_ids = jnp.arange(N_CELL, dtype=jnp.int32)[None, :]
    return jnp.where(column_ids == busy_dev, PAIR_CAP, base_count).astype(jnp.int32)


def slot_cells(key):
    slot_key = jax.random.fold_in(key, 11)
    owner_dev = jnp.arange(N_CELL * PAIR_CAP, dtype=jnp.int32)[None, :] // PAIR_CAP
    local_cell = jax.random.randint(slot_key, (N_WALL, N_CELL * PAIR_CAP), 0, CELL_DEV)
    return (owner_dev, local_cell)


def draw_pair_target(key, part):
    owner_dev, local_cell = slot_cells(key)
    return (owner_dev * CELL_DEV + local_cell).astype(jnp.int32)


def draw_pair_source(key, part):
    owner_dev, local_cell = slot_cells(key)
    half_cells = CELL_DEV // 2
    lower_side = local_cell < half_cells
    source_dev = jnp.where(lower_side, owner_dev - 1 + N_CELL, owner_dev + 1) % N_CELL
    source_local = jnp.where(lower_side, local_cell + half_cells, local_cell - half_cells)
    return (source_dev * CELL_DEV + source_local).astype(jnp.int32)


def shard_levels(stream_key, shape, shards, smallest, top_value):
    def one(position, blocks):
        steps = jax.random.uniform(jax.random.fold_in(jax.random.fold_in(stream_key, 6), position), (blocks,), jnp.float32, smallest / len(shards), top_value / len(shards))
        return jnp.repeat(jnp.exp(steps), shape[position] // blocks).reshape((-1,) + (1,) * (len(shape) - position - 1))

    level = one(*shards[0])
    for cut in shards[1:]:
        level = level * one(*cut)
    return level


def gaussian(stream_key, dims, scale, most, cuts=(), kind=jnp.bfloat16):
    values = jax.random.normal(stream_key, dims, jnp.float32) * scale
    if len(cuts) > 0:
        values = shard_levels(stream_key, dims, cuts, -0.22, 0.18) * values
    return jnp.clip(values, min=-most, max=most).astype(kind)


def setup_inputs(seed: int = 0) -> dict:
    key_of = jax.random.split(jax.random.key(seed), 10)
    self_matrix = gaussian(key_of[0], (SEG, N_WALL, 3 * PTS, 3 * PTS), (3 * PTS) ** -0.5, 0.1875, ((0, 32), (1, 8)))
    cell_source = gaussian(key_of[1], (SEG, N_WALL, 3, PTS), 1.0, 6.0, ((0, 32), (1, 8)), jnp.float32)
    cell_pos = draw_cell_pos(jax.random.fold_in(key_of[9], 71), 0)
    wall_source = gaussian(key_of[3], (3, NTH, NAX), 1.0, 6.0, ((1, 32), (2, 8)), jnp.float32)
    wall_coef = jnp.clip(jnp.exp(math.log(1.5) - 1.60943787 * jax.random.uniform(key_of[4], (NTH, NAX), jnp.float32) ** shard_levels(key_of[4], (NTH, NAX), ((0, 32), (1, 8)), -0.2, 0.2)), 0.3, 1.5)
    pair_target = draw_pair_target(jax.random.fold_in(key_of[9], 71), 0)
    pair_source = draw_pair_source(jax.random.fold_in(key_of[9], 71), 0)
    pair_count = draw_pair_count(jax.random.fold_in(key_of[9], 71), 0)
    near_wall = draw_near_wall(jax.random.fold_in(key_of[9], 71), 0)
    return {"self_matrix": self_matrix, "cell_source": cell_source, "cell_pos": cell_pos, "wall_source": wall_source, "wall_coef": wall_coef, "pair_target": pair_target, "pair_source": pair_source, "pair_count": pair_count, "near_wall": near_wall}


panel_step = 0.125
smooth_eps2 = 0.25
panel_weight = 0.015625


def panel_places(theta_idx, axial_idx, theta_total):
    radius = theta_total * panel_step / (2.0 * math.pi)
    angle_rad = (2.0 * math.pi / theta_total) * theta_idx.astype(jnp.float32)
    return jnp.stack([radius * jnp.cos(angle_rad), radius * jnp.sin(angle_rad), panel_step * axial_idx.astype(jnp.float32)])


def stokes_apply(targets, sources, density_in):
    offset_vec = targets[:, :, None] - sources[:, None, :]
    dist_sq = jnp.sum(offset_vec * offset_vec, axis=0)
    fall_off = (dist_sq + smooth_eps2) ** -1.5
    near_level = dist_sq + 2.0 * smooth_eps2
    along_vec = jnp.sum(offset_vec * density_in[:, None, :], axis=0)
    return jnp.sum((near_level * density_in[:, None, :] + along_vec * offset_vec) * fall_off, axis=2)


def wall_block(points, panels, density_in, wall_in):
    offset_vec = points[:, :, None] - panels[:, None, :]
    dist_sq = jnp.sum(offset_vec * offset_vec, axis=0)
    fall_off = (dist_sq + smooth_eps2) ** -1.5
    near_level = dist_sq + 2.0 * smooth_eps2
    along_wall = jnp.sum(offset_vec * wall_in[:, None, :], axis=0)
    to_cell = jnp.sum((near_level * wall_in[:, None, :] + along_wall * offset_vec) * fall_off, axis=2)
    along_cell = jnp.sum(offset_vec * density_in[:, :, None], axis=0)
    to_wall = jnp.sum((near_level * density_in[:, :, None] + along_cell * offset_vec) * fall_off, axis=1)
    return to_cell, to_wall


def apply_operator(density_in, wall_in, self_matrix, cell_pos, wall_coef, pair_target, pair_source, live_mask, near_wall):
    total_cells = SEG * N_WALL
    flat_matrix = self_matrix.reshape(total_cells, 3 * PTS, 3 * PTS)
    flat_dens = density_in.reshape(total_cells, 3 * PTS).astype(jnp.bfloat16)
    self_term = lax.map(lambda entry_pair: jnp.dot(entry_pair[0], entry_pair[1], preferred_element_type=jnp.float32), (flat_matrix, flat_dens))
    velocity = self_term.reshape(SEG, N_WALL, 3, PTS)

    wall_ids = jnp.broadcast_to(jnp.arange(N_WALL, dtype=jnp.int32)[:, None], pair_target.shape).reshape(-1)
    target_flat = pair_target.reshape(-1)
    source_flat = pair_source.reshape(-1)
    live_flat = live_mask.reshape(-1)

    def pair_step(entry):
        target_cell, source_cell, wall_id, live_one = entry
        pair_term = stokes_apply(cell_pos[target_cell, wall_id], cell_pos[source_cell, wall_id], density_in[source_cell, wall_id])
        return pair_term * (live_one * (8.0 / PTS))

    pair_terms = lax.map(pair_step, (target_flat, source_flat, wall_ids, live_flat))
    velocity = velocity.at[target_flat, wall_ids].add(pair_terms)

    owner_dev = (jnp.arange(SEG, dtype=jnp.int32) // CELL_DEV)[:, None, None]
    wall_row = jnp.arange(N_WALL, dtype=jnp.int32)[None, :, None]
    theta_idx = owner_dev * PAN_TH - REACH + near_wall // EXT_AX
    axial_idx = wall_row * PAN_AX - REACH + near_wall % EXT_AX
    theta_flat = theta_idx.reshape(total_cells, NEAR_PAN)
    axial_flat = axial_idx.reshape(total_cells, NEAR_PAN)
    theta_mod = theta_flat % NTH
    axial_mod = axial_flat % NAX

    def wall_step(entry):
        points, dens_one, theta_one, axial_one, theta_wrap, axial_wrap = entry
        panels = panel_places(theta_one, axial_one, NTH)
        picked = wall_in[:, theta_wrap, axial_wrap]
        to_cell, to_wall = wall_block(points, panels, dens_one, picked)
        return panel_weight * to_cell, (8.0 / PTS) * to_wall

    to_cells, to_walls = lax.map(wall_step, (cell_pos.reshape(total_cells, 3, PTS), density_in.reshape(total_cells, 3, PTS), theta_flat, axial_flat, theta_mod, axial_mod))
    velocity = velocity + to_cells.reshape(SEG, N_WALL, 3, PTS)

    stencil = jnp.roll(wall_in, 1, 1) + jnp.roll(wall_in, -1, 1) + jnp.roll(wall_in, 1, 2) + jnp.roll(wall_in, -1, 2)
    wall_vel = wall_coef * 0.25 * stencil
    spread_walls = jnp.transpose(to_walls, (1, 0, 2)).reshape(3, total_cells * NEAR_PAN)
    wall_vel = wall_vel.at[:, theta_mod.reshape(-1), axial_mod.reshape(-1)].add(spread_walls)
    return velocity, wall_vel


def reference(self_matrix, cell_source, cell_pos, wall_source, wall_coef, pair_target, pair_source, pair_count, near_wall):
    slot_rank = jnp.arange(N_CELL * PAIR_CAP, dtype=jnp.int32)[None, :] % PAIR_CAP
    live_mask = (slot_rank < jnp.repeat(pair_count, PAIR_CAP, axis=1)).astype(jnp.float32)
    velocity, wall_vel = apply_operator(cell_source, wall_source, self_matrix, cell_pos, wall_coef, pair_target, pair_source, live_mask, near_wall)
    first_cells = cell_source + velocity
    first_wall = wall_source + wall_vel
    velocity, wall_vel = apply_operator(first_cells, first_wall, self_matrix, cell_pos, wall_coef, pair_target, pair_source, live_mask, near_wall)
    return cell_source + velocity, wall_source + wall_vel
```

```python
import functools
import math

import jax
import jax.numpy as jnp
from jax import lax
from jax.experimental import pallas as pl
from jax.experimental.pallas import tpu as pltpu
from jax.sharding import PartitionSpec as P

REACH = 16
PAIR_CAP = 8
LANES = 128
ROWS = 8
BLOCK = 2 * REACH
KINDS = 16

panel_step = 0.125
smooth_eps2 = 0.25
panel_weight = 0.015625

MESH = pl.DeviceIdType.MESH
MINOR = (((1,), (1,)), ((), ()))
PLAIN = (((1,), (0,)), ((), ()))

AROUND = ((-1, 0), (1, 0), (0, -1), (0, 1), (-1, -1), (-1, 1), (1, -1), (1, 1))
F32 = jnp.float32
BF16 = jnp.bfloat16


def span(step, low, mid, high):
    return low if step < 0 else (high if step > 0 else mid)


def halves(value):
    high = value.astype(BF16)
    return high, (value - high.astype(F32)).astype(BF16)


def source_kinds(place, load):
    along = place[0] * load[0] + place[1] * load[1] + place[2] * load[2]
    norm = place[0] * place[0] + place[1] * place[1] + place[2] * place[2]
    kinds = [load[0], load[1], load[2]]
    for c in range(3):
        for i in range(3):
            kinds.append(2.0 * load[c] * place[i] + load[i] * place[c])
    for c in range(3):
        kinds.append(along * place[c] + norm * load[c])
    return kinds


def target_sum(place, sums):
    norm = place[0] * place[0] + place[1] * place[1] + place[2] * place[2]
    along = place[0] * sums[0] + place[1] * sums[1] + place[2] * sums[2]
    trace = (sums[3] + sums[7] + sums[11]) * (1.0 / 3.0)
    out = []
    for c in range(3):
        cross = place[0] * sums[3 + 3 * c] + place[1] * sums[4 + 3 * c] + place[2] * sums[5 + 3 * c]
        out.append(
            (norm + 2.0 * smooth_eps2) * sums[c] + place[c] * (along - trace) - cross + sums[12 + c]
        )
    return out


def body(
    n_cell,
    n_wall,
    near_ref,
    target_ref,
    source_ref,
    count_ref,
    matrix_hbm,
    cell_hbm,
    pos_hbm,
    wall_hbm,
    coef_hbm,
    cell_out,
    wall_out,
    matrix,
    own_pos,
    dens,
    near_pos,
    near_dens,
    coef,
    wall_ext0,
    wall_ext1,
    spill,
    from_rows,
    from_cols,
    from_corners,
    centred,
    columns,
    places,
    level,
    kinds_f32,
    kinds,
    flat_kinds,
    wall_sums,
    local_sem,
    small_send,
    small_recv,
    dens_send,
    dens_recv,
    wall_send,
    wall_recv,
    spill_send,
    spill_recv,
):
    wall_ext = (wall_ext0, wall_ext1)
    cells, _, points = own_pos.shape
    span_theta, span_axial = coef.shape
    ext_axial = span_axial + 2 * REACH
    theta_total = span_theta * n_cell
    point_tiles = points // LANES
    wall_tiles = BLOCK * BLOCK // LANES
    tiles = wall_tiles + 2 * cells * point_tiles
    pair_scale = 8.0 / points
    ext_tiles = span_axial // LANES + 2
    ext_groups = (span_theta + 2 * REACH) // ROWS
    row_groups = span_theta // ROWS + 1
    me_cell = lax.axis_index("cell")
    me_wall = lax.axis_index("wall")

    def device(step):
        return (
            lax.rem(me_cell + step[0] + n_cell, n_cell),
            lax.rem(me_wall + step[1] + n_wall, n_wall),
        )

    locals_ = []
    for number, (src, dst) in enumerate(
        [
            (pos_hbm.at[:, 0], own_pos),
            (cell_hbm.at[:, 0], dens.at[0]),
            (wall_hbm, wall_ext[0].at[:, pl.ds(REACH, span_theta), pl.ds(LANES, span_axial)]),
            (coef_hbm, coef),
        ]
        + [(matrix_hbm.at[k, 0], matrix.at[k]) for k in range(cells)]
    ):
        copy = pltpu.make_async_copy(src, dst, local_sem.at[number])
        copy.start()
        locals_.append(copy)

    barrier = pltpu.get_barrier_semaphore()
    for step in AROUND:
        pl.semaphore_signal(barrier, inc=1, device_id=device(step), device_id_type=MESH)
    pl.semaphore_wait(barrier, len(AROUND))

    def remote(src, dst, send, recv, step):
        copy = pltpu.make_async_remote_copy(
            src_ref=src, dst_ref=dst, send_sem=send, recv_sem=recv,
            device_id=device(step), device_id_type=MESH,
        )
        copy.start()
        return copy

    small = []
    for side, step in enumerate(((1, 0), (-1, 0))):
        small.append(
            remote(pos_hbm.at[:, 0], near_pos.at[side], small_send.at[0, side], small_recv.at[0, side], step)
        )
        small.append(
            remote(cell_hbm.at[:, 0], near_dens.at[0, side], small_send.at[1, side], small_recv.at[1, side], step)
        )

    def send_band(src, row_base, lane_base, which):
        out = []
        for number, step in enumerate(AROUND):
            rows = span(step[0], REACH, span_theta, REACH)
            lanes = span(step[1], LANES, span_axial, LANES)
            from_row = row_base + span(step[0], 0, 0, span_theta - REACH)
            from_lane = lane_base + span(step[1], 0, 0, span_axial - LANES)
            to_row = span(step[0], REACH + span_theta, REACH, 0)
            to_lane = span(step[1], LANES + span_axial, LANES, 0)
            out.append(
                remote(
                    src.at[:, pl.ds(from_row, rows), pl.ds(from_lane, lanes)],
                    wall_ext[which].at[:, pl.ds(to_row, rows), pl.ds(to_lane, lanes)],
                    wall_send.at[which, number],
                    wall_recv.at[which, number],
                    step,
                )
            )
        return out

    band = [send_band(wall_hbm, 0, 0, 0), None]

    lane_iota = lax.broadcasted_iota(jnp.int32, (ROWS, LANES), 1)
    row_iota = lax.broadcasted_iota(jnp.int32, (ROWS, LANES), 0)
    in_block = lane_iota % BLOCK
    block_row = row_iota + ROWS * (lane_iota // BLOCK)

    row_shift, row_group, offset, held_tile, held_chunk, theta_of, axial_of = [], [], [], [], [], [], []
    for k in range(cells):
        first = jnp.broadcast_to(near_ref[k, :, 0:1], (ROWS, LANES))
        row = ((first.astype(F32) + 0.5) * (1.0 / ext_axial)).astype(jnp.int32)
        column = first - row * ext_axial
        lane = column + (LANES - REACH)
        off = lane & (LANES - 1)
        row_shift.append(row & (ROWS - 1))
        row_group.append(row >> 3)
        offset.append(off)
        held_tile.append((lane >> 7) + jnp.where(lane_iota < off, 1, 0))
        held_chunk.append(((lane_iota - off) & (LANES - 1)) >> 5)
        theta_of.append(me_cell * span_theta - REACH + row + block_row)
        axial_of.append(me_wall * span_axial - REACH + column + in_block)

    def turn_lanes(value, amount):
        for bit in range(7):
            value = jnp.where((amount & (1 << bit)) != 0, pltpu.roll(value, 1 << bit, axis=1), value)
        return value

    def turn_rows(value, amount):
        for bit in range(3):
            value = jnp.where((amount & (1 << bit)) != 0, pltpu.roll(value, 1 << bit, axis=0), value)
        return value

    locals_[0].wait()
    locals_[1].wait()

    centre = []
    for k in range(cells):
        mid = jnp.sum(own_pos[k], axis=1, keepdims=True) * (1.0 / points)
        centre.append(mid)
        rel = own_pos[k] - mid
        centred[k] = rel
        for c in range(3):
            for j in range(point_tiles):
                piece = jnp.broadcast_to(rel[c : c + 1, j * LANES : (j + 1) * LANES], (LANES, LANES))
                columns[k, c, pl.ds(j * LANES, LANES), :] = piece.T
        theta = theta_of[k].astype(F32)
        axial = axial_of[k].astype(F32)
        angle = (2.0 * math.pi / theta_total) * theta
        radius = theta_total * panel_step / (2.0 * math.pi)
        places[k, 0, pl.ds(0, ROWS), :] = radius * jnp.cos(angle) - mid[0:1]
        places[k, 1, pl.ds(0, ROWS), :] = radius * jnp.sin(angle) - mid[1:2]
        places[k, 2, pl.ds(0, ROWS), :] = panel_step * axial - mid[2:3]

    def fill_level(k, first, last):
        def one(tile, carry):
            y = [
                jnp.broadcast_to(places[k, c, pl.ds(tile, 1), :], (BLOCK // 2, LANES))
                for c in range(3)
            ]
            lanes = pl.ds(pl.multiple_of(tile * LANES, LANES), LANES)
            for g in range(points // 16):
                rows = pl.ds(16 * g, 16)
                dx = columns[k, 0, rows, :] - y[0]
                dy = columns[k, 1, rows, :] - y[1]
                dz = columns[k, 2, rows, :] - y[2]
                inverse = lax.rsqrt(dx * dx + dy * dy + dz * dz + smooth_eps2)
                high, low = halves(inverse * inverse * inverse)
                level[k, rows, lanes] = high
                level[k, pl.ds(points + 16 * g, 16), lanes] = low
            return carry

        lax.fori_loop(first, last, one, 0)

    for k in range(cells):
        fill_level(k, 0, wall_tiles)

    def to_wall(turn):
        blocks = []
        for k in range(cells):
            rel = centred[k]
            load = dens[turn, k] * pair_scale
            rows = source_kinds(
                [rel[c : c + 1] for c in range(3)], [load[c : c + 1] for c in range(3)]
            )
            rows.append(jnp.zeros_like(rows[0]))
            high, low = halves(jnp.concatenate(rows, axis=0))
            flat_kinds[pl.ds(0, KINDS), pl.ds(0, points)] = high
            flat_kinds[pl.ds(0, KINDS), pl.ds(points, points)] = high
            flat_kinds[pl.ds(KINDS, KINDS), pl.ds(0, points)] = low
            flat_kinds[pl.ds(KINDS, KINDS), pl.ds(points, points)] = low
            sums = lax.dot_general(
                flat_kinds[...], level[k, :, pl.ds(0, wall_tiles * LANES)], PLAIN,
                preferred_element_type=F32,
            )
            sums = sums[:KINDS] + sums[KINDS:]
            for a in range(wall_tiles):
                wall_sums[k, pl.ds(a * KINDS, KINDS), :] = sums[:, a * LANES : (a + 1) * LANES]
            by_kind = [wall_sums[k, pl.ds(n, wall_tiles, stride=KINDS), :] for n in range(15)]
            place = [places[k, c, pl.ds(0, ROWS), :] for c in range(3)]
            found = target_sum(place, by_kind)
            shift, group = row_shift[k], row_group[k]
            laid = []
            for c in range(3):
                turned = turn_rows(turn_lanes(found[c], offset[k]), shift)
                parts = [
                    jnp.where(held_chunk[k] == 0, pltpu.roll(turned, LANES - BLOCK * b, axis=1) if b else turned, 0.0)
                    for b in range(BLOCK // ROWS)
                ]
                steps = []
                for j in range(BLOCK // ROWS + 1):
                    low = parts[j] if j < len(parts) else jnp.zeros_like(turned)
                    high = parts[j - 1] if j > 0 else jnp.zeros_like(turned)
                    steps.append(jnp.where(row_iota >= shift, low, high))
                rows_ = []
                for g in range(ext_groups):
                    value = jnp.zeros_like(turned)
                    for r in range(row_groups):
                        if 0 <= g - r < len(steps):
                            value = jnp.where(group == r, steps[g - r], value)
                    rows_.append(value)
                laid.append(rows_)
            blocks.append(laid)
        for t in range(ext_tiles):
            here = [held_tile[k] == t for k in range(cells)]
            for c in range(3):
                for g in range(ext_groups):
                    total = jnp.where(here[0], blocks[0][c][g], 0.0)
                    for k in range(1, cells):
                        total = total + jnp.where(here[k], blocks[k][c][g], 0.0)
                    spill[turn, c, pl.ds(ROWS * g, ROWS), pl.ds(t * LANES, LANES)] = total
        out = []
        for number, step in enumerate(AROUND):
            rows = span(step[0], REACH, span_theta, REACH)
            lanes = span(step[1], LANES, span_axial, LANES)
            from_row = span(step[0], 0, REACH, REACH + span_theta)
            from_lane = span(step[1], 0, LANES, LANES + span_axial)
            if step[1] == 0:
                dst = from_rows.at[turn, number]
            elif step[0] == 0:
                dst = from_cols.at[turn, number - 2]
            else:
                dst = from_corners.at[turn, number - 4]
            out.append(
                remote(
                    spill.at[turn, :, pl.ds(from_row, rows), pl.ds(from_lane, lanes)],
                    dst,
                    spill_send.at[turn, number],
                    spill_recv.at[turn, number],
                    step,
                )
            )
        return out

    spills = [to_wall(0), None]

    def self_term(turn, k):
        flat = jnp.concatenate([dens[turn, k, c : c + 1] for c in range(3)], axis=1)
        rows = jnp.broadcast_to(flat, (16, flat.shape[1])).astype(BF16)
        found = lax.dot_general(rows, matrix[k], MINOR, preferred_element_type=F32)
        return jnp.concatenate([found[0:1, c * points : (c + 1) * points] for c in range(3)], axis=0)

    for k in range(cells):
        locals_[4 + k].wait()
    velocity = [self_term(0, k) for k in range(cells)]

    slots = target_ref.shape[1]
    slot = lax.broadcasted_iota(jnp.int32, (1, slots), 1)
    device_lane = lax.broadcasted_iota(jnp.int32, count_ref.shape, 1)
    live = jnp.sum(jnp.where(device_lane == me_cell, count_ref[...], 0).astype(F32), axis=1, keepdims=True)
    first_slot = me_cell * PAIR_CAP
    in_use = (slot >= first_slot) & ((slot - first_slot).astype(F32) < live)
    sides = (lax.rem(me_cell + n_cell - 1, n_cell), lax.rem(me_cell + 1, n_cell))
    weight = []
    for k in range(cells):
        mine = in_use & (target_ref[...] == me_cell * cells + k)
        weight.append(
            [
                jnp.sum(
                    jnp.where(mine & (source_ref[...] == sides[s // cells] * cells + s % cells), pair_scale, 0.0),
                    axis=1,
                    keepdims=True,
                )
                for s in range(2 * cells)
            ]
        )

    for copy in small:
        copy.wait_recv()
    for k in range(cells):
        for s in range(2 * cells):
            rel = near_pos[s // cells, s % cells] - centre[k]
            for c in range(3):
                for j in range(point_tiles):
                    places[k, c, pl.ds(wall_tiles + s * point_tiles + j, 1), :] = rel[
                        c : c + 1, j * LANES : (j + 1) * LANES
                    ]
    for k in range(cells):
        fill_level(k, wall_tiles, tiles)

    def stencil(which):
        found = []
        for c in range(3):
            mid = wall_ext[which][c, pl.ds(REACH, span_theta), :]
            width = mid.shape[1]
            sides = pltpu.roll(mid, 1, axis=1) + pltpu.roll(mid, width - 1, axis=1)
            up = wall_ext[which][c, pl.ds(REACH + 1, span_theta), pl.ds(LANES, span_axial)]
            down = wall_ext[which][c, pl.ds(REACH - 1, span_theta), pl.ds(LANES, span_axial)]
            found.append(
                coef[...] * 0.25 * (up + down + sides[:, LANES : LANES + span_axial])
            )
        return found

    def wait_band(which):
        for copy in band[which]:
            copy.wait_recv()

    locals_[2].wait()
    locals_[3].wait()
    wait_band(0)
    first_wall = wall_ext[1].at[:, pl.ds(REACH, span_theta), pl.ds(LANES, span_axial)]
    found = stencil(0)
    for c in range(3):
        first_wall[c] = (
            wall_ext[0][c, pl.ds(REACH, span_theta), pl.ds(LANES, span_axial)]
            + found[c]
            + spill[0, c, pl.ds(REACH, span_theta), pl.ds(LANES, span_axial)]
        )
    for copy in spills[0]:
        copy.wait_recv()

    def add_fold(turn, out_ref):
        for number, step in enumerate(AROUND):
            rows = span(step[0], REACH, span_theta, REACH)
            lanes = span(step[1], LANES, span_axial, LANES)
            to_row = span(step[0], span_theta - REACH, 0, 0)
            to_lane = span(step[1], span_axial - LANES, 0, 0)
            if step[1] == 0:
                piece = from_rows[turn, number]
            elif step[0] == 0:
                piece = from_cols[turn, number - 2]
            else:
                piece = from_corners[turn, number - 4]
            view = out_ref.at[:, pl.ds(to_row, rows), pl.ds(to_lane, lanes)]
            view[...] = view[...] + piece

    add_fold(0, first_wall)
    band[1] = send_band(wall_ext[1], REACH, LANES, 1)

    def to_cell(turn, k):
        loads = []
        for c in range(3):
            rows_ = []
            for g in range(ext_groups):
                value = None
                for t in range(ext_tiles):
                    piece = wall_ext[turn][c, pl.ds(ROWS * g, ROWS), pl.ds(t * LANES, LANES)]
                    value = piece if t == 0 else jnp.where(held_tile[k] == t, piece, value)
                rows_.append(value)
            steps = []
            for j in range(BLOCK // ROWS + 1):
                value = rows_[j]
                for r in range(1, row_groups):
                    if j + r < ext_groups:
                        value = jnp.where(row_group[k] == r, rows_[j + r], value)
                steps.append(turn_rows(value, ROWS - row_shift[k]))
            packed = None
            for b in range(BLOCK // ROWS):
                part = jnp.where(row_iota + row_shift[k] < ROWS, steps[b], steps[b + 1])
                part = pltpu.roll(part, BLOCK * b, axis=1) if b else part
                packed = jnp.where(held_chunk[k] == b, part, packed) if b else part
            picked = turn_lanes(packed, LANES - offset[k])
            rest = []
            for s in range(2 * cells):
                for j in range(point_tiles):
                    rest.append(
                        near_dens[turn, s // cells, s % cells, c : c + 1, j * LANES : (j + 1) * LANES]
                        * weight[k][s]
                    )
            rest += [jnp.zeros((1, LANES), F32)] * (places.shape[2] - tiles)
            loads.append(jnp.concatenate([picked * panel_weight] + rest, axis=0))
        place = [places[k, c] for c in range(3)]
        held = source_kinds(place, loads)
        for n in range(15):
            kinds_f32[pl.ds(n, places.shape[2], stride=KINDS), :] = held[n]
        for a in range(tiles):
            high, low = halves(kinds_f32[pl.ds(a * KINDS, KINDS), :])
            kinds[pl.ds(0, KINDS), pl.ds(a * LANES, LANES)] = high
            kinds[pl.ds(KINDS, KINDS), pl.ds(a * LANES, LANES)] = low
        sums = lax.dot_general(kinds[...], level[k], MINOR, preferred_element_type=F32)
        sums = sums[:KINDS] + sums[KINDS:]
        sums = sums[:, :points] + sums[:, points:]
        rel = centred[k]
        found = target_sum(
            [rel[c : c + 1] for c in range(3)], [sums[n : n + 1] for n in range(15)]
        )
        return jnp.concatenate(found, axis=0)

    kinds_f32[...] = jnp.zeros(kinds_f32.shape, F32)
    for k in range(cells):
        for c in range(3):
            places[k, c, pl.ds(tiles, places.shape[2] - tiles), :] = jnp.zeros(
                (places.shape[2] - tiles, LANES), F32
            )

    for k in range(cells):
        dens[1, k] = dens[0, k] + velocity[k] + to_cell(0, k)

    later = []
    for side, step in enumerate(((1, 0), (-1, 0))):
        later.append(
            remote(dens.at[1], near_dens.at[1, side], dens_send.at[side], dens_recv.at[side], step)
        )

    spills[1] = to_wall(1)
    velocity = [self_term(1, k) for k in range(cells)]

    wait_band(1)
    found = stencil(1)
    for c in range(3):
        wall_out[c] = (
            wall_ext[0][c, pl.ds(REACH, span_theta), pl.ds(LANES, span_axial)]
            + found[c]
            + spill[1, c, pl.ds(REACH, span_theta), pl.ds(LANES, span_axial)]
        )
    for copy in later:
        copy.wait_recv()
    for k in range(cells):
        cell_out[k, 0] = dens[0, k] + velocity[k] + to_cell(1, k)
    for copy in spills[1]:
        copy.wait_recv()
    add_fold(1, wall_out)

    for copy in small + band[0] + band[1] + spills[0] + spills[1] + later:
        copy.wait_send()


def local(
    n_cell, n_wall,
    self_matrix, cell_source, cell_pos, wall_source, wall_coef, pair_target, pair_source, pair_count, near_wall,
):
    cells, _, _, points = cell_pos.shape
    _, span_theta, span_axial = wall_source.shape
    unknowns = self_matrix.shape[-1]
    wall_tiles = BLOCK * BLOCK // LANES
    tiles = wall_tiles + 2 * cells * (points // LANES)
    rows = -(-tiles // ROWS) * ROWS
    ext_rows = span_theta + 2 * REACH
    ext_lanes = span_axial + 2 * LANES
    vmem = lambda *shape: pltpu.VMEM(shape, F32)
    dma = lambda *shape: pltpu.SemaphoreType.DMA(shape)
    hbm = pl.BlockSpec(memory_space=pl.ANY)
    full = pl.BlockSpec(memory_space=pltpu.VMEM)
    return pl.pallas_call(
        functools.partial(body, n_cell, n_wall),
        out_shape=(
            jax.ShapeDtypeStruct(cell_source.shape, F32),
            jax.ShapeDtypeStruct(wall_source.shape, F32),
        ),
        in_specs=[full] * 4 + [hbm] * 5,
        out_specs=(full, full),
        scratch_shapes=[
            pltpu.VMEM((cells, unknowns, unknowns), BF16),
            vmem(cells, 3, points),
            vmem(2, cells, 3, points),
            vmem(2, cells, 3, points),
            vmem(2, 2, cells, 3, points),
            vmem(span_theta, span_axial),
            vmem(3, ext_rows, ext_lanes),
            vmem(3, ext_rows, ext_lanes),
            vmem(2, 3, ext_rows, ext_lanes),
            vmem(2, 2, 3, REACH, span_axial),
            vmem(2, 2, 3, span_theta, LANES),
            vmem(2, 4, 3, REACH, LANES),
            vmem(cells, 3, points),
            vmem(cells, 3, points, LANES),
            vmem(cells, 3, rows, LANES),
            pltpu.VMEM((cells, 2 * points, tiles * LANES), BF16),
            vmem(rows * KINDS, LANES),
            pltpu.VMEM((2 * KINDS, tiles * LANES), BF16),
            pltpu.VMEM((2 * KINDS, 2 * points), BF16),
            vmem(cells, wall_tiles * KINDS, LANES),
            dma(4 + cells),
            dma(2, 2),
            dma(2, 2),
            dma(2),
            dma(2),
            dma(2, 8),
            dma(2, 8),
            dma(2, 8),
            dma(2, 8),
        ],
        compiler_params=pltpu.CompilerParams(
            collective_id=0, has_side_effects=True, vmem_limit_bytes=48 * 2**20
        ),
        cost_estimate=pl.CostEstimate(flops=2 * 10**9, bytes_accessed=8 * 10**6, transcendentals=2 * 10**6),
        name="picard",
    )(
        near_wall, pair_target, pair_source, pair_count,
        self_matrix, cell_source, cell_pos, wall_source, wall_coef,
    )


def solution(mesh):
    placed = (
        P("cell", "wall", None, None),
        P("cell", "wall", None, None),
        P("cell", "wall", None, None),
        P(None, "cell", "wall"),
        P("cell", "wall"),
        P("wall", None),
        P("wall", None),
        P("wall", None),
        P("cell", "wall", None),
    )
    return jax.shard_map(
        functools.partial(local, mesh.shape["cell"], mesh.shape["wall"]),
        mesh=mesh,
        in_specs=placed,
        out_specs=(P("cell", "wall", None, None), P(None, "cell", "wall")),
        check_vma=False,
    )
```

```python
import functools
import math

import jax
import jax.numpy as jnp
from jax import lax
from jax.experimental import pallas as pl
from jax.experimental.pallas import tpu as pltpu
from jax.sharding import PartitionSpec as P

REACH = 16
PAIR_CAP = 8
LANES = 128
ROWS = 8
BLOCK = 2 * REACH
KINDS = 16

panel_step = 0.125
smooth_eps2 = 0.25
panel_weight = 0.015625

MESH = pl.DeviceIdType.MESH
MINOR = (((1,), (1,)), ((), ()))
PLAIN = (((1,), (0,)), ((), ()))

AROUND = ((-1, 0), (1, 0), (0, -1), (0, 1), (-1, -1), (-1, 1), (1, -1), (1, 1))
F32 = jnp.float32
BF16 = jnp.bfloat16


def span(step, low, mid, high):
    return low if step < 0 else (high if step > 0 else mid)


def halves(value):
    high = value.astype(BF16)
    return high, (value - high.astype(F32)).astype(BF16)


def source_kinds(place, load):
    along = place[0] * load[0] + place[1] * load[1] + place[2] * load[2]
    norm = place[0] * place[0] + place[1] * place[1] + place[2] * place[2]
    kinds = [load[0], load[1], load[2]]
    for c in range(3):
        for i in range(3):
            kinds.append(2.0 * load[c] * place[i] + load[i] * place[c])
    for c in range(3):
        kinds.append(along * place[c] + norm * load[c])
    return kinds


def target_sum(place, sums):
    norm = place[0] * place[0] + place[1] * place[1] + place[2] * place[2]
    along = place[0] * sums[0] + place[1] * sums[1] + place[2] * sums[2]
    trace = (sums[3] + sums[7] + sums[11]) * (1.0 / 3.0)
    out = []
    for c in range(3):
        cross = place[0] * sums[3 + 3 * c] + place[1] * sums[4 + 3 * c] + place[2] * sums[5 + 3 * c]
        out.append(
            (norm + 2.0 * smooth_eps2) * sums[c] + place[c] * (along - trace) - cross + sums[12 + c]
        )
    return out


def three(value):
    high = value.astype(BF16).astype(F32)
    rest = value - high
    mid = rest.astype(BF16).astype(F32)
    return high, mid, rest - mid


def square_sides(place, of_target):
    norm = place[0] * place[0] + place[1] * place[1] + place[2] * place[2]
    one = jnp.ones_like(norm)
    rows = []
    for c in range(3):
        high, mid, low = three(place[c] if of_target else -2.0 * place[c])
        rows += [high, high, mid, high, low, mid] if of_target else [high, mid, high, low, high, mid]
    if of_target:
        return rows + [*three(norm + smooth_eps2), one, one, one]
    return rows + [one, one, one, *three(norm)]


def body(
    n_cell,
    n_wall,
    near_hbm,
    target_hbm,
    source_hbm,
    count_hbm,
    matrix_hbm,
    cell_hbm,
    pos_hbm,
    wall_hbm,
    coef_hbm,
    cell_out,
    wall_out,
    matrix,
    state,
    near_state,
    dens1,
    near_dens1,
    coef,
    wall_ext0,
    wall_ext1,
    spill0,
    spill1,
    got_spill,
    pack,
    got_pack,
    near_own,
    near_got,
    target_row,
    source_row,
    count_row,
    columns,
    sources,
    places,
    level,
    square_f32,
    kinds_f32,
    kinds,
    flat_kinds,
    wall_sums,
    spread,
    gather,
    every,
    unturn,
    turn_spread,
    replica,
    held_groups,
    local_sem,
    state_send,
    state_recv,
    dens_send,
    dens_recv,
    near_send,
    near_recv,
    wall_send,
    wall_recv,
    edge_send,
    edge_recv,
    pack_send,
    pack_recv,
    spill_send,
    spill_recv,
):
    cells, points = matrix.shape[0], state.shape[-1]
    span_theta, span_axial = coef.shape
    ext_axial = span_axial + 2 * REACH
    theta_total = span_theta * n_cell
    point_tiles = points // LANES
    wall_tiles = BLOCK * BLOCK // LANES
    tiles = wall_tiles + 2 * cells * point_tiles
    tile_rows = places.shape[2]
    pair_scale = 8.0 / points
    own_tiles = span_axial // LANES
    ext_tiles = own_tiles + 2
    ext_groups = (span_theta + 2 * REACH) // ROWS
    row_groups = span_theta // ROWS + 1
    chunks = BLOCK // ROWS
    pairs_of_groups = ext_groups // 2
    spill = (spill0, spill1)
    me_cell = lax.axis_index("cell")
    me_wall = lax.axis_index("wall")

    def device(step):
        return (
            lax.rem(me_cell + step[0] + n_cell, n_cell),
            lax.rem(me_wall + step[1] + n_wall, n_wall),
        )

    own_near = near_hbm.at[:, :, pl.ds(0, LANES)]
    inside = []
    for number, (src, dst) in enumerate(
        [
            (pos_hbm, state.at[0]),
            (cell_hbm, state.at[1]),
            (own_near, near_own),
            (wall_hbm, wall_ext0.at[:, pl.ds(REACH, span_theta), pl.ds(LANES, span_axial)]),
            (coef_hbm, coef),
            (target_hbm, target_row),
            (source_hbm, source_row),
            (count_hbm, count_row),
        ]
        + [(matrix_hbm.at[k, 0], matrix.at[k]) for k in range(cells)]
    ):
        copy = pltpu.make_async_copy(src, dst, local_sem.at[number])
        copy.start()
        inside.append(copy)

    barrier = pltpu.get_barrier_semaphore()
    for step in AROUND:
        pl.semaphore_signal(barrier, inc=1, device_id=device(step), device_id_type=MESH)

    def remote(src, dst, send, recv, step):
        copy = pltpu.make_async_remote_copy(
            src_ref=src, dst_ref=dst, send_sem=send, recv_sem=recv,
            device_id=device(step), device_id_type=MESH,
        )
        copy.start()
        return copy

    lane_iota = lax.broadcasted_iota(jnp.int32, (ROWS, LANES), 1)
    row_iota = lax.broadcasted_iota(jnp.int32, (ROWS, LANES), 0)
    chunk_iota = lane_iota // BLOCK
    in_block = lane_iota % BLOCK
    block_row = row_iota + ROWS * chunk_iota
    nothing = jnp.zeros((ROWS, LANES), F32)

    in_chunk = lane_iota % BLOCK

    class Block:
        def __init__(self, first):
            first = jnp.broadcast_to(first, (ROWS, LANES))
            self.row = ((first.astype(F32) + 0.5) * (1.0 / ext_axial)).astype(jnp.int32)
            self.column = first - self.row * ext_axial
            lane = self.column + (LANES - REACH)
            self.turn = lane & (BLOCK - 1)
            self.shift = self.row & (ROWS - 1)
            self.group = self.row >> 3
            self.where = (lane >> 5) + jnp.where(in_chunk < self.turn, 1, 0) - chunk_iota

    def turn_rows(value, amount):
        for bit in range(3):
            value = jnp.where((amount & (1 << bit)) != 0, pltpu.roll(value, 1 << bit, axis=0), value)
        return value

    def moved(values, matrix_, dims=PLAIN):
        count = values.shape[0]
        terms = jnp.concatenate(three(values), axis=0).astype(BF16)
        out = lax.dot_general(terms, matrix_, dims, preferred_element_type=F32)
        return out[:count] + out[count : 2 * count] + out[2 * count :]

    def stacked(values):
        return jnp.concatenate(values, axis=0)

    def zero_one(mask):
        return jnp.where(mask, 1.0, 0.0).astype(BF16)

    from_lane = lax.broadcasted_iota(jnp.int32, (LANES, LANES), 0)
    to_lane_ = lax.broadcasted_iota(jnp.int32, (LANES, LANES), 1)
    same = (from_lane & (BLOCK - 1)) == (to_lane_ & (BLOCK - 1))
    every[...] = zero_one(same)
    for q in range(chunks):
        spread[:, pl.ds(q * LANES, LANES)] = zero_one(same & (from_lane >> 5 == q))
        gather[pl.ds(q * LANES, LANES), :] = zero_one(same & (to_lane_ >> 5 == q))

    square_f32[...] = jnp.zeros(square_f32.shape, F32)
    kinds_f32[...] = jnp.zeros(kinds_f32.shape, F32)
    sources[...] = jnp.zeros(sources.shape, BF16)

    inside[0].wait()
    inside[1].wait()
    inside[2].wait()
    own_block = [Block(near_own[k, :, 0:1]) for k in range(cells)]
    for k in range(cells):
        turn = jnp.broadcast_to(own_block[k].turn[0:1], (LANES, LANES))
        same = ((from_lane + turn) & (BLOCK - 1)) == (to_lane_ & (BLOCK - 1))
        unturn[k] = zero_one(same & (from_lane >> 5 == to_lane_ >> 5))
        for q in range(chunks):
            turn_spread[k, :, pl.ds(q * LANES, LANES)] = zero_one(same & (from_lane >> 5 == q))

    def rows_of(ref, k):
        return [ref[k, c] for c in range(3)]

    def fill_sources(k, first, count):
        place = [places[k, c, pl.ds(first, count), :] for c in range(3)]
        for n, value in enumerate(square_sides(place, False)):
            square_f32[pl.ds(first * BLOCK + n, count, stride=BLOCK), :] = value
        for a in range(first, min(first + count, tiles)):
            sources[k, pl.ds(0, BLOCK), pl.ds(a * LANES, LANES)] = square_f32[
                pl.ds(a * BLOCK, BLOCK), :
            ].astype(BF16)

    def fill_level(k, first, last):
        def one(step, carry):
            lanes = pl.ds(pl.multiple_of(step * 2 * LANES, 2 * LANES), 2 * LANES)
            square = lax.dot_general(columns[k], sources[k, :, lanes], PLAIN, preferred_element_type=F32)
            inverse = lax.rsqrt(square)
            high, low = halves(inverse * inverse * inverse)
            level[k, pl.ds(0, points), lanes] = high
            level[k, pl.ds(points, points), lanes] = low
            return carry

        lax.fori_loop(first // 2, last // 2, one, 0)

    centre, centred = [], []
    for k in range(cells):
        own = rows_of(state.at[0], k)
        mid = [jnp.sum(own[c], axis=1, keepdims=True) * (1.0 / points) for c in range(3)]
        rel = [own[c] - mid[c] for c in range(3)]
        centre.append(mid)
        centred.append(rel)
        rows = square_sides(rel, True)
        rows = jnp.concatenate(rows + [jnp.zeros((LANES - len(rows), points), F32)], axis=0)
        for j in range(point_tiles):
            columns[k, pl.ds(j * LANES, LANES), :] = rows[:, j * LANES : (j + 1) * LANES].T.astype(BF16)
        theta = (me_cell * span_theta - REACH + own_block[k].row + block_row).astype(F32)
        axial = (me_wall * span_axial - REACH + own_block[k].column + in_block).astype(F32)
        angle = (2.0 * math.pi / theta_total) * theta
        radius = theta_total * panel_step / (2.0 * math.pi)
        places[k, 0, pl.ds(0, ROWS), :] = radius * jnp.cos(angle) - mid[0]
        places[k, 1, pl.ds(0, ROWS), :] = radius * jnp.sin(angle) - mid[1]
        places[k, 2, pl.ds(0, ROWS), :] = panel_step * axial - mid[2]
        for c in range(3):
            places[k, c, pl.ds(tiles, tile_rows - tiles), :] = jnp.zeros((tile_rows - tiles, LANES), F32)
        fill_sources(k, 0, wall_tiles)
        fill_level(k, 0, wall_tiles)

    def to_wall(turn):
        merged = [[nothing] * 3 for _ in range(pairs_of_groups)]
        for k in range(cells):
            load = rows_of(state.at[1] if turn == 0 else dens1, k)
            rows = source_kinds(centred[k], [value * pair_scale for value in load])
            rows.append(jnp.zeros_like(rows[0]))
            high, low = halves(jnp.concatenate(rows, axis=0))
            flat_kinds[pl.ds(0, KINDS), pl.ds(0, points)] = high
            flat_kinds[pl.ds(0, KINDS), pl.ds(points, points)] = high
            flat_kinds[pl.ds(KINDS, KINDS), pl.ds(0, points)] = low
            flat_kinds[pl.ds(KINDS, KINDS), pl.ds(points, points)] = low
            sums = lax.dot_general(
                flat_kinds[...], level[k, :, pl.ds(0, wall_tiles * LANES)], PLAIN,
                preferred_element_type=F32,
            )
            sums = sums[:KINDS] + sums[KINDS:]
            for a in range(wall_tiles):
                wall_sums[k, pl.ds(a * KINDS, KINDS), :] = sums[:, a * LANES : (a + 1) * LANES]
            by_kind = [wall_sums[k, pl.ds(n, wall_tiles, stride=KINDS), :] for n in range(15)]
            found = target_sum([places[k, c, pl.ds(0, ROWS), :] for c in range(3)], by_kind)
            block = own_block[k]
            parts = moved(stacked([turn_rows(value, block.shift) for value in found]), turn_spread[k])
            for c in range(3):
                part = [
                    parts[c * ROWS : (c + 1) * ROWS, q * LANES : (q + 1) * LANES] for q in range(chunks)
                ]
                steps = [
                    jnp.where(
                        row_iota >= block.shift,
                        part[j] if j < chunks else nothing,
                        part[j - 1] if j else nothing,
                    )
                    for j in range(chunks + 1)
                ]
                for g in range(ext_groups):
                    value = nothing
                    for r in range(row_groups):
                        if 0 <= g - r <= chunks:
                            value = jnp.where(block.group == r, steps[g - r], value)
                    merged[g // 2][c] = jnp.where(chunk_iota == 2 * k + g % 2, value, merged[g // 2][c])
        for v in range(pairs_of_groups):
            for c in range(3):
                spill[turn][v, c] = merged[v][c]

    def cut_of(step):
        return span(step[0], (0, 1), (1, 2), (3, 1))

    def send_spill(turn):
        out = []
        for number, step in enumerate(AROUND):
            first, count = cut_of(step)
            out.append(
                remote(
                    spill[turn].at[pl.ds(first, count)],
                    got_spill.at[turn, number, pl.ds(0, count)],
                    spill_send.at[turn, number],
                    spill_recv.at[turn, number],
                    step,
                )
            )
        return out

    to_wall(0)
    pl.semaphore_wait(barrier, len(AROUND))

    beside = [
        remote(state, near_state.at[side], state_send.at[side], state_recv.at[side], step)
        for side, step in enumerate(((1, 0), (-1, 0)))
    ]
    band = []
    for number, step in enumerate(AROUND):
        rows = span(step[0], REACH, span_theta, REACH)
        lanes = span(step[1], LANES, span_axial, LANES)
        from_row = span(step[0], 0, 0, span_theta - REACH)
        from_lane = span(step[1], 0, 0, span_axial - LANES)
        to_row = span(step[0], REACH + span_theta, REACH, 0)
        to_lane = span(step[1], LANES + span_axial, LANES, 0)
        band.append(
            remote(
                wall_hbm.at[:, pl.ds(from_row, rows), pl.ds(from_lane, lanes)],
                wall_ext0.at[:, pl.ds(to_row, rows), pl.ds(to_lane, lanes)],
                wall_send.at[number],
                wall_recv.at[number],
                step,
            )
        )
    around = [
        remote(own_near, near_got.at[number], near_send.at[number], near_recv.at[number], step)
        for number, step in enumerate(AROUND)
    ]
    spills = [send_spill(0), None]

    def self_term(turn, k):
        flat = jnp.concatenate(rows_of(state.at[1] if turn == 0 else dens1, k), axis=1)
        rows = jnp.broadcast_to(flat, (16, flat.shape[1])).astype(BF16)
        found = lax.dot_general(rows, matrix[k], MINOR, preferred_element_type=F32)
        return [found[0:1, c * points : (c + 1) * points] for c in range(3)]

    for copy in inside[3:]:
        copy.wait()
    velocity = [self_term(0, k) for k in range(cells)]

    slots = target_row.shape[1]
    slot = lax.broadcasted_iota(jnp.int32, (1, slots), 1)
    device_lane = lax.broadcasted_iota(jnp.int32, count_row.shape, 1)
    live = jnp.sum(jnp.where(device_lane == me_cell, count_row[...], 0).astype(F32), axis=1, keepdims=True)
    first_slot = me_cell * PAIR_CAP
    in_use = (slot >= first_slot) & ((slot - first_slot).astype(F32) < live)
    sides = (lax.rem(me_cell + n_cell - 1, n_cell), lax.rem(me_cell + 1, n_cell))
    weight = []
    for k in range(cells):
        mine = in_use & (target_row[...] == me_cell * cells + k)
        weight.append(
            [
                jnp.sum(
                    jnp.where(mine & (source_row[...] == sides[s // cells] * cells + s % cells), pair_scale, 0.0),
                    axis=1,
                    keepdims=True,
                )
                for s in range(2 * cells)
            ]
        )

    for copy in beside:
        copy.wait_recv()
    for k in range(cells):
        for s in range(2 * cells):
            for c in range(3):
                rel = near_state[s // cells, 0, s % cells, c] - centre[k][c]
                for j in range(point_tiles):
                    places[k, c, pl.ds(wall_tiles + s * point_tiles + j, 1), :] = rel[
                        :, j * LANES : (j + 1) * LANES
                    ]
        fill_sources(k, wall_tiles, tile_rows - wall_tiles)
        fill_level(k, wall_tiles, tiles)

    def add_spill(turn, view):
        for half in range(2):
            origins = [(spill[turn], 1 + half, own_where, 0)]
            for number, step in enumerate(AROUND):
                if step[0] == 0:
                    origins.append((got_spill.at[turn, number], half, got_where[number], step[1]))
                elif (step[0] > 0) == (half == 0):
                    origins.append((got_spill.at[turn, number], 0, got_where[number], step[1]))
            replica[pl.ds(0, len(origins) * 3 * ROWS), :] = moved(
                stacked([ref[v, c] for ref, v, _, _ in origins for c in range(3)]), spread[...]
            )
            for t in range(own_tiles):
                sums = {}
                for o, (_, _, blocks, aside) in enumerate(origins):
                    if aside and t != (0 if aside > 0 else own_tiles - 1):
                        continue
                    for k in range(cells):
                        mask = blocks[k] == chunks * (t + 1 + own_tiles * aside)
                        for c in range(3):
                            for g in range(2):
                                part = replica[
                                    pl.ds((3 * o + c) * ROWS, ROWS), pl.ds((2 * k + g) * LANES, LANES)
                                ]
                                part = jnp.where(mask, part, 0.0)
                                sums[c, g] = sums[c, g] + part if (c, g) in sums else part
                for (c, g), value in sums.items():
                    spot = view.at[c, pl.ds(2 * ROWS * half + ROWS * g, ROWS), pl.ds(t * LANES, LANES)]
                    spot[...] = spot[...] + value

    def stencil(ref):
        found = []
        for c in range(3):
            mid = ref[c, pl.ds(REACH, span_theta), :]
            width = mid.shape[1]
            sides_ = pltpu.roll(mid, 1, axis=1) + pltpu.roll(mid, width - 1, axis=1)
            up = ref[c, pl.ds(REACH + 1, span_theta), pl.ds(LANES, span_axial)]
            down = ref[c, pl.ds(REACH - 1, span_theta), pl.ds(LANES, span_axial)]
            found.append(coef[...] * 0.25 * (up + down + sides_[:, LANES : LANES + span_axial]))
        return found

    def block_loads(groups, k):
        block = own_block[k]
        out = []
        for c in range(3):
            steps = []
            for j in range(chunks + 1):
                value = groups(c, j)
                for r in range(1, row_groups):
                    if j + r < ext_groups:
                        value = jnp.where(block.group == r, groups(c, j + r), value)
                steps.append(turn_rows(value, ROWS - block.shift))
            packed = nothing
            for b in range(chunks):
                part = jnp.where(row_iota + block.shift < ROWS, steps[b], steps[b + 1])
                packed = jnp.where(chunk_iota == b, part, packed)
            out.append(packed)
        out = moved(stacked(out), unturn[k], MINOR)
        return [out[c * ROWS : (c + 1) * ROWS] for c in range(3)]

    def to_cell(turn, k, picked):
        loads = []
        for c in range(3):
            rest = []
            for s in range(2 * cells):
                if turn == 0:
                    beside_load = near_state[s // cells, 1, s % cells, c]
                else:
                    beside_load = near_dens1[s // cells, s % cells, c]
                beside_load = beside_load * weight[k][s]
                for j in range(point_tiles):
                    rest.append(beside_load[:, j * LANES : (j + 1) * LANES])
            rest += [jnp.zeros((1, LANES), F32)] * (tile_rows - tiles)
            loads.append(jnp.concatenate([picked[c] * panel_weight] + rest, axis=0))
        held = source_kinds([places[k, c] for c in range(3)], loads)
        for n in range(15):
            kinds_f32[pl.ds(n, tile_rows, stride=KINDS), :] = held[n]
        for a in range(tiles):
            high, low = halves(kinds_f32[pl.ds(a * KINDS, KINDS), :])
            kinds[pl.ds(0, KINDS), pl.ds(a * LANES, LANES)] = high
            kinds[pl.ds(KINDS, KINDS), pl.ds(a * LANES, LANES)] = low
        sums = lax.dot_general(kinds[...], level[k], MINOR, preferred_element_type=F32)
        sums = sums[:KINDS] + sums[KINDS:]
        sums = sums[:, :points] + sums[:, points:]
        return target_sum(centred[k], [sums[n : n + 1] for n in range(15)])

    for copy in band:
        copy.wait_recv()
    centre_rows = pl.ds(REACH, span_theta)
    centre_lanes = pl.ds(LANES, span_axial)
    first_wall = wall_ext1.at[:, centre_rows, centre_lanes]
    found = stencil(wall_ext0)
    for c in range(3):
        first_wall[c] = wall_ext0[c, centre_rows, centre_lanes] + found[c]
    for copy in around + spills[0]:
        copy.wait_recv()
    got_where = [[Block(near_got[number, k, :, 0:1]).where for k in range(cells)] for number in range(len(AROUND))]
    own_where = [own_block[k].where for k in range(cells)]
    add_spill(0, first_wall)

    units = [(number, v, first) for number, step in enumerate(AROUND)
             for v, first in enumerate(span(step[0], (0,), (0, 2), (2,)))]
    units += [(None, 0, 0), (None, 1, 2)]
    for u, (number, v, first) in enumerate(units):
        step = (0, 0) if number is None else AROUND[number]
        blocks = own_where if number is None else got_where[AROUND.index((-step[0], -step[1]))]
        held = span(step[1], [0], range(own_tiles), [own_tiles - 1])
        for k in range(cells):
            masks = [(t, blocks[k] == chunks * (t + 1 - own_tiles * step[1])) for t in held]
            for c in range(3):
                for g in range(2):
                    rows = pl.ds(REACH + ROWS * (first + g), ROWS)
                    one = nothing
                    for t, mask in masks:
                        one = jnp.where(mask, wall_ext1[c, rows, pl.ds((t + 1) * LANES, LANES)], one)
                    replica[pl.ds((3 * u + c) * ROWS, ROWS), pl.ds((2 * k + g) * LANES, LANES)] = one
    packed = moved(replica[...], gather[...])
    for u, (number, v, first) in enumerate(units):
        for c in range(3):
            pack[len(AROUND) if number is None else number, v, c] = packed[(3 * u + c) * ROWS : (3 * u + c + 1) * ROWS]
    packs = []
    for number, step in enumerate(AROUND):
        count = 2 if step[0] == 0 else 1
        packs.append(
            remote(
                pack.at[number, pl.ds(0, count)],
                got_pack.at[number, pl.ds(0, count)],
                pack_send.at[number],
                pack_recv.at[number],
                step,
            )
        )

    def band_loads(k):
        masks = [own_where[k] == chunks * t for t in range(ext_tiles)]
        for c in range(3):
            for g in range(ext_groups):
                value = nothing
                for t in range(ext_tiles):
                    piece = wall_ext0[c, pl.ds(ROWS * g, ROWS), pl.ds(t * LANES, LANES)]
                    value = jnp.where(masks[t], piece, value)
                held_groups[pl.ds((c * ext_groups + g) * ROWS, ROWS), :] = value
        held_groups[...] = moved(held_groups[...], every[...])
        return block_loads(lambda c, g: held_groups[pl.ds((c * ext_groups + g) * ROWS, ROWS), :], k)

    for k in range(cells):
        found = to_cell(0, k, band_loads(k))
        for c in range(3):
            dens1[k, c] = state[1, k, c] + velocity[k][c] + found[c]

    later = [
        remote(dens1, near_dens1.at[side], dens_send.at[side], dens_recv.at[side], step)
        for side, step in enumerate(((1, 0), (-1, 0)))
    ]
    to_wall(1)
    spills[1] = send_spill(1)

    edge = []
    for number, step in enumerate(AROUND[:4]):
        rows = span(step[0], ROWS, span_theta, ROWS)
        lanes = span(step[1], LANES, span_axial, LANES)
        from_row = REACH + span(step[0], 0, 0, span_theta - ROWS)
        from_lane = LANES + span(step[1], 0, 0, span_axial - LANES)
        to_row = span(step[0], REACH + span_theta, REACH, REACH - ROWS)
        to_lane = span(step[1], LANES + span_axial, LANES, 0)
        edge.append(
            remote(
                wall_ext1.at[:, pl.ds(from_row, rows), pl.ds(from_lane, lanes)],
                wall_ext1.at[:, pl.ds(to_row, rows), pl.ds(to_lane, lanes)],
                edge_send.at[number],
                edge_recv.at[number],
                step,
            )
        )

    velocity = [self_term(1, k) for k in range(cells)]

    for copy in packs:
        copy.wait_recv()
    cut = [[nothing] * 3 for _ in range(pairs_of_groups)]
    for v in range(2):
        for c in range(3):
            cut[1 + v][c] = pack[len(AROUND), v, c]
    for number, step in enumerate(AROUND):
        first, count = span(step[0], (3, 1), (1, 2), (0, 1))
        for v in range(count):
            for c in range(3):
                cut[first + v][c] = cut[first + v][c] + got_pack[number, v, c]
    cut_rows = 3 * pairs_of_groups * ROWS
    replica[pl.ds(0, cut_rows), :] = moved(stacked([value for per in cut for value in per]), spread[...])

    def pack_loads(k):
        return block_loads(
            lambda c, g: replica[
                pl.ds((g // 2 * 3 + c) * ROWS, ROWS), pl.ds((2 * k + g % 2) * LANES, LANES)
            ],
            k,
        )

    for copy in later:
        copy.wait_recv()
    for k in range(cells):
        found = to_cell(1, k, pack_loads(k))
        for c in range(3):
            cell_out[k, c] = state[1, k, c] + velocity[k][c] + found[c]

    for copy in edge:
        copy.wait_recv()
    found = stencil(wall_ext1)
    for c in range(3):
        wall_out[c] = wall_ext0[c, centre_rows, centre_lanes] + found[c]
    for copy in spills[1]:
        copy.wait_recv()
    add_spill(1, wall_out)

    for copy in beside + band + around + spills[0] + packs + later + spills[1] + edge:
        copy.wait_send()


def local(
    n_cell, n_wall,
    self_matrix, cell_source, cell_pos, wall_source, wall_coef, pair_target, pair_source, pair_count, near_wall,
):
    cells, _, _, points = cell_pos.shape
    _, span_theta, span_axial = wall_source.shape
    unknowns = self_matrix.shape[-1]
    wall_tiles = BLOCK * BLOCK // LANES
    tiles = wall_tiles + 2 * cells * (points // LANES)
    rows = -(-tiles // ROWS) * ROWS
    ext_rows = span_theta + 2 * REACH
    ext_lanes = span_axial + 2 * LANES
    vmem = lambda *shape: pltpu.VMEM(shape, F32)
    ints = lambda *shape: pltpu.VMEM(shape, jnp.int32)
    dma = lambda *shape: pltpu.SemaphoreType.DMA(shape)
    hbm = pl.BlockSpec(memory_space=pl.ANY)
    full = pl.BlockSpec(memory_space=pltpu.VMEM)
    by_component = (cells, 3, 1, points)
    velocity, wall = pl.pallas_call(
        functools.partial(body, n_cell, n_wall),
        out_shape=(
            jax.ShapeDtypeStruct(by_component, F32),
            jax.ShapeDtypeStruct(wall_source.shape, F32),
        ),
        in_specs=[hbm] * 9,
        out_specs=(full, full),
        scratch_shapes=[
            pltpu.VMEM((cells, unknowns, unknowns), BF16),
            vmem(2, *by_component),
            vmem(2, 2, *by_component),
            vmem(*by_component),
            vmem(2, *by_component),
            vmem(span_theta, span_axial),
            vmem(3, ext_rows, ext_lanes),
            vmem(3, ext_rows, ext_lanes),
            vmem(4, 3, ROWS, LANES),
            vmem(4, 3, ROWS, LANES),
            vmem(2, 8, 2, 3, ROWS, LANES),
            vmem(9, 2, 3, ROWS, LANES),
            vmem(8, 2, 3, ROWS, LANES),
            ints(cells, 1, LANES),
            ints(8, cells, 1, LANES),
            ints(*pair_target.shape),
            ints(*pair_source.shape),
            ints(*pair_count.shape),
            pltpu.VMEM((cells, points, LANES), BF16),
            pltpu.VMEM((cells, LANES, tiles * LANES), BF16),
            vmem(cells, 3, rows, LANES),
            pltpu.VMEM((cells, 2 * points, tiles * LANES), BF16),
            vmem(rows * BLOCK, LANES),
            vmem(rows * KINDS, LANES),
            pltpu.VMEM((2 * KINDS, tiles * LANES), BF16),
            pltpu.VMEM((2 * KINDS, 2 * points), BF16),
            vmem(cells, wall_tiles * KINDS, LANES),
            pltpu.VMEM((LANES, 4 * LANES), BF16),
            pltpu.VMEM((4 * LANES, LANES), BF16),
            pltpu.VMEM((LANES, LANES), BF16),
            pltpu.VMEM((cells, LANES, LANES), BF16),
            pltpu.VMEM((cells, LANES, 4 * LANES), BF16),
            vmem(12 * 3 * ROWS, 4 * LANES),
            vmem(3 * ext_rows, LANES),
            dma(8 + cells),
            dma(2),
            dma(2),
            dma(2),
            dma(2),
            dma(8),
            dma(8),
            dma(8),
            dma(8),
            dma(4),
            dma(4),
            dma(8),
            dma(8),
            dma(2, 8),
            dma(2, 8),
        ],
        compiler_params=pltpu.CompilerParams(
            collective_id=0, has_side_effects=True, vmem_limit_bytes=60 * 2**20
        ),
        cost_estimate=pl.CostEstimate(flops=2 * 10**9, bytes_accessed=8 * 10**6, transcendentals=2 * 10**6),
        name="picard",
    )(
        near_wall, pair_target, pair_source, pair_count,
        self_matrix, cell_source.transpose(0, 2, 1, 3), cell_pos.transpose(0, 2, 1, 3), wall_source, wall_coef,
    )
    return velocity.transpose(0, 2, 1, 3), wall


def solution(mesh):
    placed = (
        P("cell", "wall", None, None),
        P("cell", "wall", None, None),
        P("cell", "wall", None, None),
        P(None, "cell", "wall"),
        P("cell", "wall"),
        P("wall", None),
        P("wall", None),
        P("wall", None),
        P("cell", "wall", None),
    )
    return jax.shard_map(
        functools.partial(local, mesh.shape["cell"], mesh.shape["wall"]),
        mesh=mesh,
        in_specs=placed,
        out_specs=(P("cell", "wall", None, None), P(None, "cell", "wall")),
        check_vma=False,
    )
```

```python
import functools
import math

import jax
import jax.numpy as jnp
from jax import lax
from jax.experimental import pallas as pl
from jax.experimental.pallas import tpu as pltpu
from jax.sharding import PartitionSpec as P

REACH = 16
PAIR_CAP = 8
LANES = 128
ROWS = 8
BLOCK = 2 * REACH
KINDS = 16

panel_step = 0.125
smooth_eps2 = 0.25
panel_weight = 0.015625

MESH = pl.DeviceIdType.MESH
MINOR = (((1,), (1,)), ((), ()))
PLAIN = (((1,), (0,)), ((), ()))

AROUND = ((-1, 0), (1, 0), (0, -1), (0, 1), (-1, -1), (-1, 1), (1, -1), (1, 1))
F32 = jnp.float32
BF16 = jnp.bfloat16


def span(step, low, mid, high):
    return low if step < 0 else (high if step > 0 else mid)


def halves(value):
    high = value.astype(BF16)
    return high, (value - high.astype(F32)).astype(BF16)


def source_kinds(place, load):
    along = place[0] * load[0] + place[1] * load[1] + place[2] * load[2]
    norm = place[0] * place[0] + place[1] * place[1] + place[2] * place[2]
    kinds = [load[0], load[1], load[2]]
    for c in range(3):
        for i in range(3):
            kinds.append(2.0 * load[c] * place[i] + load[i] * place[c])
    for c in range(3):
        kinds.append(along * place[c] + norm * load[c])
    return kinds


def target_sum(place, sums):
    norm = place[0] * place[0] + place[1] * place[1] + place[2] * place[2]
    along = place[0] * sums[0] + place[1] * sums[1] + place[2] * sums[2]
    trace = (sums[3] + sums[7] + sums[11]) * (1.0 / 3.0)
    out = []
    for c in range(3):
        cross = place[0] * sums[3 + 3 * c] + place[1] * sums[4 + 3 * c] + place[2] * sums[5 + 3 * c]
        out.append(
            (norm + 2.0 * smooth_eps2) * sums[c] + place[c] * (along - trace) - cross + sums[12 + c]
        )
    return out


def three(value):
    high = value.astype(BF16).astype(F32)
    rest = value - high
    mid = rest.astype(BF16).astype(F32)
    return high, mid, rest - mid


def square_sides(place, of_target):
    norm = place[0] * place[0] + place[1] * place[1] + place[2] * place[2]
    one = jnp.ones_like(norm)
    rows = []
    for c in range(3):
        high, mid, low = three(place[c] if of_target else -2.0 * place[c])
        rows += [high, high, mid, high, low, mid] if of_target else [high, mid, high, low, high, mid]
    if of_target:
        return rows + [*three(norm + smooth_eps2), one, one, one]
    return rows + [one, one, one, *three(norm)]


def body(
    n_cell,
    n_wall,
    near_hbm,
    target_hbm,
    source_hbm,
    count_hbm,
    matrix_hbm,
    cell_hbm,
    pos_hbm,
    wall_hbm,
    coef_hbm,
    cell_out,
    wall_out,
    matrix,
    state,
    near_state,
    dens1,
    near_dens1,
    coef,
    wall_ext0,
    wall_ext1,
    spill0,
    spill1,
    got_spill0,
    got_spill1,
    pack,
    got_pack,
    near_own,
    target_row,
    source_row,
    count_row,
    columns,
    sources,
    places,
    level,
    square_f32,
    kinds_f32,
    kinds,
    flat_kinds,
    wall_sums,
    spread,
    gather,
    every,
    unturn,
    turn_spread,
    replica,
    held_groups,
    local_sem,
    state_send,
    state_recv,
    dens_send,
    dens_recv,
    wall_send,
    wall_recv,
    edge_send,
    edge_recv,
    pack_send,
    pack_recv,
    spill_send,
    spill_recv,
):
    cells, points = matrix.shape[0], state.shape[-1]
    span_theta, span_axial = coef.shape
    ext_axial = span_axial + 2 * REACH
    theta_total = span_theta * n_cell
    point_tiles = points // LANES
    wall_tiles = BLOCK * BLOCK // LANES
    tiles = wall_tiles + 2 * cells * point_tiles
    tile_rows = places.shape[2]
    pair_scale = 8.0 / points
    own_tiles = span_axial // LANES
    ext_tiles = own_tiles + 2
    ext_groups = (span_theta + 2 * REACH) // ROWS
    row_groups = span_theta // ROWS + 1
    chunks = BLOCK // ROWS
    pairs_of_groups = ext_groups // 2
    spill, got_spill = (spill0, spill1), (got_spill0, got_spill1)
    me_cell = lax.axis_index("cell")
    me_wall = lax.axis_index("wall")

    def device(step):
        return (
            lax.rem(me_cell + step[0] + n_cell, n_cell),
            lax.rem(me_wall + step[1] + n_wall, n_wall),
        )

    barrier = pltpu.get_barrier_semaphore()
    for step in AROUND:
        pl.semaphore_signal(barrier, inc=1, device_id=device(step), device_id_type=MESH)

    own_near = near_hbm.at[:, :, pl.ds(0, LANES)]
    inside = []
    for number, (src, dst) in enumerate(
        [
            (pos_hbm, state.at[0]),
            (cell_hbm, state.at[1]),
            (own_near, near_own),
            (wall_hbm, wall_ext0.at[:, pl.ds(REACH, span_theta), pl.ds(LANES, span_axial)]),
            (coef_hbm, coef),
            (target_hbm, target_row),
            (source_hbm, source_row),
            (count_hbm, count_row),
        ]
        + [(matrix_hbm.at[k, 0], matrix.at[k]) for k in range(cells)]
    ):
        copy = pltpu.make_async_copy(src, dst, local_sem.at[number])
        copy.start()
        inside.append(copy)

    def remote(src, dst, send, recv, step):
        copy = pltpu.make_async_remote_copy(
            src_ref=src, dst_ref=dst, send_sem=send, recv_sem=recv,
            device_id=device(step), device_id_type=MESH,
        )
        copy.start()
        return copy

    lane_iota = lax.broadcasted_iota(jnp.int32, (ROWS, LANES), 1)
    row_iota = lax.broadcasted_iota(jnp.int32, (ROWS, LANES), 0)
    chunk_iota = lane_iota // BLOCK
    in_block = lane_iota % BLOCK
    block_row = row_iota + ROWS * chunk_iota
    nothing = jnp.zeros((ROWS, LANES), F32)

    in_chunk = lane_iota % BLOCK

    class Block:
        def __init__(self, first):
            first = jnp.broadcast_to(first, (ROWS, LANES))
            self.row = ((first.astype(F32) + 0.5) * (1.0 / ext_axial)).astype(jnp.int32)
            self.column = first.astype(jnp.int32) - self.row * ext_axial
            lane = self.column + (LANES - REACH)
            self.turn = lane & (BLOCK - 1)
            self.shift = self.row & (ROWS - 1)
            self.group = self.row >> 3
            self.where = (lane >> 5) + jnp.where(in_chunk < self.turn, 1, 0) - chunk_iota

    def turn_rows(value, amount):
        for bit in range(3):
            value = jnp.where((amount & (1 << bit)) != 0, pltpu.roll(value, 1 << bit, axis=0), value)
        return value

    def moved(values, matrix_, dims=PLAIN):
        count = values.shape[0]
        terms = jnp.concatenate(three(values), axis=0).astype(BF16)
        out = lax.dot_general(terms, matrix_, dims, preferred_element_type=F32)
        return out[:count] + out[count : 2 * count] + out[2 * count :]

    def stacked(values):
        return jnp.concatenate(values, axis=0)

    def zero_one(mask):
        return jnp.where(mask, 1.0, 0.0).astype(BF16)

    from_lane = lax.broadcasted_iota(jnp.int32, (LANES, LANES), 0)
    to_lane_ = lax.broadcasted_iota(jnp.int32, (LANES, LANES), 1)
    same = (from_lane & (BLOCK - 1)) == (to_lane_ & (BLOCK - 1))
    every[...] = zero_one(same)
    for q in range(chunks):
        spread[:, pl.ds(q * LANES, LANES)] = zero_one(same & (from_lane >> 5 == q))
        gather[pl.ds(q * LANES, LANES), :] = zero_one(same & (to_lane_ >> 5 == q))

    square_f32[...] = jnp.zeros(square_f32.shape, F32)
    kinds_f32[...] = jnp.zeros(kinds_f32.shape, F32)

    inside[0].wait()
    inside[1].wait()
    inside[2].wait()
    own_block = [Block(near_own[k, :, 0:1]) for k in range(cells)]
    width = LANES // cells
    own_first = nothing
    for k in range(cells):
        own_first = jnp.where(lane_iota // width == k, near_own[k, :, 0:1].astype(F32), own_first)
    for k in range(cells):
        turn = jnp.broadcast_to(own_block[k].turn[0:1], (LANES, LANES))
        same = ((from_lane + turn) & (BLOCK - 1)) == (to_lane_ & (BLOCK - 1))
        unturn[k] = zero_one(same & (from_lane >> 5 == to_lane_ >> 5))
        for q in range(chunks):
            turn_spread[k, :, pl.ds(q * LANES, LANES)] = zero_one(same & (from_lane >> 5 == q))

    def rows_of(ref, k):
        return [ref[k, c] for c in range(3)]

    def fill_sources(k, first, count):
        place = [places[k, c, pl.ds(first, count), :] for c in range(3)]
        for n, value in enumerate(square_sides(place, False)):
            square_f32[pl.ds(first * BLOCK + n, count, stride=BLOCK), :] = value
        for a in range(first, min(first + count, tiles)):
            sources[k, :, pl.ds(a * LANES, LANES)] = square_f32[
                pl.ds(a * BLOCK, BLOCK), :
            ].astype(BF16)

    def fill_level(k, first, last):
        def one(step, carry):
            lanes = pl.ds(pl.multiple_of(step * 2 * LANES, 2 * LANES), 2 * LANES)
            square = lax.dot_general(columns[k, :, pl.ds(0, BLOCK)], sources[k, :, lanes], PLAIN, preferred_element_type=F32)
            inverse = lax.rsqrt(square)
            high, low = halves(inverse * inverse * inverse)
            level[k, pl.ds(0, points), lanes] = high
            level[k, pl.ds(points, points), lanes] = low
            return carry

        lax.fori_loop(first // 2, last // 2, one, 0, unroll=True)

    centre, centred = [], []
    for k in range(cells):
        own = rows_of(state.at[0], k)
        mid = [jnp.sum(own[c], axis=1, keepdims=True) * (1.0 / points) for c in range(3)]
        rel = [own[c] - mid[c] for c in range(3)]
        centre.append(mid)
        centred.append(rel)
        rows = square_sides(rel, True)
        rows = jnp.concatenate(rows + [jnp.zeros((LANES - len(rows), points), F32)], axis=0)
        for j in range(point_tiles):
            columns[k, pl.ds(j * LANES, LANES), :] = rows[:, j * LANES : (j + 1) * LANES].T.astype(BF16)
        theta = (me_cell * span_theta - REACH + own_block[k].row + block_row).astype(F32)
        axial = (me_wall * span_axial - REACH + own_block[k].column + in_block).astype(F32)
        angle = (2.0 * math.pi / theta_total) * theta
        radius = theta_total * panel_step / (2.0 * math.pi)
        places[k, 0, pl.ds(0, ROWS), :] = radius * jnp.cos(angle) - mid[0]
        places[k, 1, pl.ds(0, ROWS), :] = radius * jnp.sin(angle) - mid[1]
        places[k, 2, pl.ds(0, ROWS), :] = panel_step * axial - mid[2]
        for c in range(3):
            places[k, c, pl.ds(tiles, tile_rows - tiles), :] = jnp.zeros((tile_rows - tiles, LANES), F32)
        fill_sources(k, 0, wall_tiles)
        fill_level(k, 0, wall_tiles)

    def to_wall(turn):
        merged = [[nothing] * 3 for _ in range(pairs_of_groups)]
        for k in range(cells):
            load = rows_of(state.at[1] if turn == 0 else dens1, k)
            rows = source_kinds(centred[k], [value * pair_scale for value in load])
            rows.append(jnp.zeros_like(rows[0]))
            high, low = halves(jnp.concatenate(rows, axis=0))
            flat_kinds[pl.ds(0, KINDS), pl.ds(0, points)] = high
            flat_kinds[pl.ds(0, KINDS), pl.ds(points, points)] = high
            flat_kinds[pl.ds(KINDS, KINDS), pl.ds(0, points)] = low
            flat_kinds[pl.ds(KINDS, KINDS), pl.ds(points, points)] = low
            sums = lax.dot_general(
                flat_kinds[...], level[k, :, pl.ds(0, wall_tiles * LANES)], PLAIN,
                preferred_element_type=F32,
            )
            sums = sums[:KINDS] + sums[KINDS:]
            for a in range(wall_tiles):
                wall_sums[k, pl.ds(a * KINDS, KINDS), :] = sums[:, a * LANES : (a + 1) * LANES]
            by_kind = [wall_sums[k, pl.ds(n, wall_tiles, stride=KINDS), :] for n in range(15)]
            found = target_sum([places[k, c, pl.ds(0, ROWS), :] for c in range(3)], by_kind)
            block = own_block[k]
            parts = moved(stacked([turn_rows(value, block.shift) for value in found]), turn_spread[k])
            for c in range(3):
                part = [
                    parts[c * ROWS : (c + 1) * ROWS, q * LANES : (q + 1) * LANES] for q in range(chunks)
                ]
                steps = [
                    jnp.where(
                        row_iota >= block.shift,
                        part[j] if j < chunks else nothing,
                        part[j - 1] if j else nothing,
                    )
                    for j in range(chunks + 1)
                ]
                for g in range(ext_groups):
                    value = nothing
                    for r in range(row_groups):
                        if 0 <= g - r <= chunks:
                            value = jnp.where(block.group == r, steps[g - r], value)
                    merged[g // 2][c] = jnp.where(chunk_iota == 2 * k + g % 2, value, merged[g // 2][c])
        for v in range(pairs_of_groups):
            for c in range(3):
                spill[turn][v, c] = merged[v][c]
            if turn == 0:
                spill[turn][v, 3] = own_first

    def cut_of(step):
        return span(step[0], (0, 1), (1, 2), (3, 1))

    def send_spill(turn):
        out = []
        for number, step in enumerate(AROUND):
            first, count = cut_of(step)
            out.append(
                remote(
                    spill[turn].at[pl.ds(first, count)],
                    got_spill[turn].at[number, pl.ds(0, count)],
                    spill_send.at[turn, number],
                    spill_recv.at[turn, number],
                    step,
                )
            )
        return out

    to_wall(0)
    pl.semaphore_wait(barrier, len(AROUND))

    beside = [
        remote(state, near_state.at[side], state_send.at[side], state_recv.at[side], step)
        for side, step in enumerate(((1, 0), (-1, 0)))
    ]
    spills = [send_spill(0), None]
    band = []
    for number, step in enumerate(AROUND):
        rows = span(step[0], REACH, span_theta, REACH)
        lanes = span(step[1], LANES, span_axial, LANES)
        from_row = span(step[0], 0, 0, span_theta - REACH)
        from_lane = span(step[1], 0, 0, span_axial - LANES)
        to_row = span(step[0], REACH + span_theta, REACH, 0)
        to_lane = span(step[1], LANES + span_axial, LANES, 0)
        band.append(
            remote(
                wall_hbm.at[:, pl.ds(from_row, rows), pl.ds(from_lane, lanes)],
                wall_ext0.at[:, pl.ds(to_row, rows), pl.ds(to_lane, lanes)],
                wall_send.at[number],
                wall_recv.at[number],
                step,
            )
        )

    def self_term(turn, k):
        flat = jnp.concatenate(rows_of(state.at[1] if turn == 0 else dens1, k), axis=1)
        rows = jnp.broadcast_to(flat, (16, flat.shape[1])).astype(BF16)
        found = lax.dot_general(rows, matrix[k], MINOR, preferred_element_type=F32)
        return [found[0:1, c * points : (c + 1) * points] for c in range(3)]

    for copy in inside[3:]:
        copy.wait()
    velocity = [self_term(0, k) for k in range(cells)]

    slots = target_row.shape[1]
    slot = lax.broadcasted_iota(jnp.int32, (1, slots), 1)
    device_lane = lax.broadcasted_iota(jnp.int32, count_row.shape, 1)
    live = jnp.sum(jnp.where(device_lane == me_cell, count_row[...], 0).astype(F32), axis=1, keepdims=True)
    first_slot = me_cell * PAIR_CAP
    in_use = (slot >= first_slot) & ((slot - first_slot).astype(F32) < live)
    sides = (lax.rem(me_cell + n_cell - 1, n_cell), lax.rem(me_cell + 1, n_cell))
    weight = []
    for k in range(cells):
        mine = in_use & (target_row[...] == me_cell * cells + k)
        weight.append(
            [
                jnp.sum(
                    jnp.where(mine & (source_row[...] == sides[s // cells] * cells + s % cells), pair_scale, 0.0),
                    axis=1,
                    keepdims=True,
                )
                for s in range(2 * cells)
            ]
        )

    for copy in beside:
        copy.wait_recv()
    for k in range(cells):
        for s in range(2 * cells):
            for c in range(3):
                rel = near_state[s // cells, 0, s % cells, c] - centre[k][c]
                for j in range(point_tiles):
                    places[k, c, pl.ds(wall_tiles + s * point_tiles + j, 1), :] = rel[
                        :, j * LANES : (j + 1) * LANES
                    ]
        fill_sources(k, wall_tiles, tile_rows - wall_tiles)
        fill_level(k, wall_tiles, tiles)

    def add_spill(turn, view):
        for half in range(2):
            origins = [(spill[turn], 1 + half, own_where, 0)]
            for number, step in enumerate(AROUND):
                if step[0] == 0:
                    origins.append((got_spill[turn].at[number], half, got_where[number], step[1]))
                elif (step[0] > 0) == (half == 0):
                    origins.append((got_spill[turn].at[number], 0, got_where[number], step[1]))
            replica[pl.ds(0, len(origins) * 3 * ROWS), :] = moved(
                stacked([ref[v, c] for ref, v, _, _ in origins for c in range(3)]), spread[...]
            )
            for t in range(own_tiles):
                sums = {}
                for o, (_, _, blocks, aside) in enumerate(origins):
                    if aside and t != (0 if aside > 0 else own_tiles - 1):
                        continue
                    for k in range(cells):
                        mask = blocks[k] == chunks * (t + 1 + own_tiles * aside)
                        for c in range(3):
                            for g in range(2):
                                part = replica[
                                    pl.ds((3 * o + c) * ROWS, ROWS), pl.ds((2 * k + g) * LANES, LANES)
                                ]
                                part = jnp.where(mask, part, 0.0)
                                sums[c, g] = sums[c, g] + part if (c, g) in sums else part
                for (c, g), value in sums.items():
                    spot = view.at[c, pl.ds(2 * ROWS * half + ROWS * g, ROWS), pl.ds(t * LANES, LANES)]
                    spot[...] = spot[...] + value

    def stencil(ref):
        found = []
        for c in range(3):
            mid = ref[c, pl.ds(REACH, span_theta), :]
            width = mid.shape[1]
            sides_ = pltpu.roll(mid, 1, axis=1) + pltpu.roll(mid, width - 1, axis=1)
            up = ref[c, pl.ds(REACH + 1, span_theta), pl.ds(LANES, span_axial)]
            down = ref[c, pl.ds(REACH - 1, span_theta), pl.ds(LANES, span_axial)]
            found.append(coef[...] * 0.25 * (up + down + sides_[:, LANES : LANES + span_axial]))
        return found

    def block_loads(groups, k):
        block = own_block[k]
        out = []
        for c in range(3):
            steps = []
            for j in range(chunks + 1):
                value = groups(c, j)
                for r in range(1, row_groups):
                    if j + r < ext_groups:
                        value = jnp.where(block.group == r, groups(c, j + r), value)
                steps.append(turn_rows(value, ROWS - block.shift))
            packed = nothing
            for b in range(chunks):
                part = jnp.where(row_iota + block.shift < ROWS, steps[b], steps[b + 1])
                packed = jnp.where(chunk_iota == b, part, packed)
            out.append(packed)
        out = moved(stacked(out), unturn[k], MINOR)
        return [out[c * ROWS : (c + 1) * ROWS] for c in range(3)]

    def cell_sums(k, first, last, loads):
        count = loads[0].shape[0]
        held = source_kinds([places[k, c, pl.ds(first, count), :] for c in range(3)], loads)
        for n in range(15):
            kinds_f32[pl.ds(first * KINDS + n, count, stride=KINDS), :] = held[n]
        for a in range(first, last):
            high, low = halves(kinds_f32[pl.ds(a * KINDS, KINDS), :])
            kinds[pl.ds(0, KINDS), pl.ds(a * LANES, LANES)] = high
            kinds[pl.ds(KINDS, KINDS), pl.ds(a * LANES, LANES)] = low
        lanes = pl.ds(first * LANES, (last - first) * LANES)
        sums = lax.dot_general(kinds[:, lanes], level[k, :, lanes], MINOR, preferred_element_type=F32)
        sums = sums[:KINDS] + sums[KINDS:]
        return sums[:, :points] + sums[:, points:]

    def pair_sums(turn, k):
        loads = []
        for c in range(3):
            rest = []
            for s in range(2 * cells):
                if turn == 0:
                    beside_load = near_state[s // cells, 1, s % cells, c]
                else:
                    beside_load = near_dens1[s // cells, s % cells, c]
                beside_load = beside_load * weight[k][s]
                for j in range(point_tiles):
                    rest.append(beside_load[:, j * LANES : (j + 1) * LANES])
            rest += [jnp.zeros((1, LANES), F32)] * (tile_rows - tiles)
            loads.append(jnp.concatenate(rest, axis=0))
        return cell_sums(k, wall_tiles, tiles, loads)

    def near_sums(k, picked):
        return cell_sums(k, 0, wall_tiles, [value * panel_weight for value in picked])

    def to_cell(k, sums):
        return target_sum(centred[k], [sums[n : n + 1] for n in range(15)])

    from_pairs = [pair_sums(0, k) for k in range(cells)]

    for copy in band:
        copy.wait_recv()
    centre_rows = pl.ds(REACH, span_theta)
    centre_lanes = pl.ds(LANES, span_axial)
    first_wall = wall_ext1.at[:, centre_rows, centre_lanes]
    found = stencil(wall_ext0)
    for c in range(3):
        first_wall[c] = wall_ext0[c, centre_rows, centre_lanes] + found[c]
    for copy in spills[0]:
        copy.wait_recv()
    got_where = [
        [Block(got_spill0[number, 0, 3, 0:1, k * width : k * width + 1]).where for k in range(cells)]
        for number in range(len(AROUND))
    ]
    own_where = [own_block[k].where for k in range(cells)]
    add_spill(0, first_wall)

    units = [(number, v, first) for number, step in enumerate(AROUND)
             for v, first in enumerate(span(step[0], (0,), (0, 2), (2,)))]
    own_units = [(None, 0, 0), (None, 1, 2)]

    def make_packs(units, base):
        for u, (number, v, first) in enumerate(units):
            step = (0, 0) if number is None else AROUND[number]
            blocks = own_where if number is None else got_where[AROUND.index((-step[0], -step[1]))]
            held = span(step[1], [0], range(own_tiles), [own_tiles - 1])
            for k in range(cells):
                masks = [(t, blocks[k] == chunks * (t + 1 - own_tiles * step[1])) for t in held]
                for c in range(3):
                    for g in range(2):
                        rows = pl.ds(REACH + ROWS * (first + g), ROWS)
                        one = nothing
                        for t, mask in masks:
                            one = jnp.where(mask, wall_ext1[c, rows, pl.ds((t + 1) * LANES, LANES)], one)
                        replica[pl.ds(base + (3 * u + c) * ROWS, ROWS), pl.ds((2 * k + g) * LANES, LANES)] = one
        packed = moved(replica[pl.ds(base, 3 * ROWS * len(units)), :], gather[...])
        for u, (number, v, first) in enumerate(units):
            for c in range(3):
                spot = len(AROUND) if number is None else number
                pack[spot, v, c] = packed[(3 * u + c) * ROWS : (3 * u + c + 1) * ROWS]

    make_packs(units, 0)
    packs = []
    for number, step in enumerate(AROUND):
        count = 2 if step[0] == 0 else 1
        packs.append(
            remote(
                pack.at[number, pl.ds(0, count)],
                got_pack.at[number, pl.ds(0, count)],
                pack_send.at[number],
                pack_recv.at[number],
                step,
            )
        )

    def band_loads(k):
        masks = [own_where[k] == chunks * t for t in range(ext_tiles)]
        for c in range(3):
            for g in range(ext_groups):
                value = nothing
                for t in range(ext_tiles):
                    piece = wall_ext0[c, pl.ds(ROWS * g, ROWS), pl.ds(t * LANES, LANES)]
                    value = jnp.where(masks[t], piece, value)
                held_groups[pl.ds((c * ext_groups + g) * ROWS, ROWS), :] = value
        held_groups[...] = moved(held_groups[...], every[...])
        return block_loads(lambda c, g: held_groups[pl.ds((c * ext_groups + g) * ROWS, ROWS), :], k)

    for k in range(cells):
        found = to_cell(k, from_pairs[k] + near_sums(k, band_loads(k)))
        for c in range(3):
            dens1[k, c] = state[1, k, c] + velocity[k][c] + found[c]

    later = [
        remote(dens1, near_dens1.at[side], dens_send.at[side], dens_recv.at[side], step)
        for side, step in enumerate(((1, 0), (-1, 0)))
    ]
    to_wall(1)
    spills[1] = send_spill(1)

    edge = []
    for number, step in enumerate(AROUND[:4]):
        rows = span(step[0], ROWS, span_theta, ROWS)
        lanes = span(step[1], LANES, span_axial, LANES)
        from_row = REACH + span(step[0], 0, 0, span_theta - ROWS)
        from_lane = LANES + span(step[1], 0, 0, span_axial - LANES)
        to_row = span(step[0], REACH + span_theta, REACH, REACH - ROWS)
        to_lane = span(step[1], LANES + span_axial, LANES, 0)
        edge.append(
            remote(
                wall_ext1.at[:, pl.ds(from_row, rows), pl.ds(from_lane, lanes)],
                wall_ext1.at[:, pl.ds(to_row, rows), pl.ds(to_lane, lanes)],
                edge_send.at[number],
                edge_recv.at[number],
                step,
            )
        )

    make_packs(own_units, 3 * ROWS * len(units))
    velocity = [self_term(1, k) for k in range(cells)]

    for copy in packs:
        copy.wait_recv()
    cut = [[nothing] * 3 for _ in range(pairs_of_groups)]
    for v in range(2):
        for c in range(3):
            cut[1 + v][c] = pack[len(AROUND), v, c]
    for number, step in enumerate(AROUND):
        first, count = span(step[0], (3, 1), (1, 2), (0, 1))
        for v in range(count):
            for c in range(3):
                cut[first + v][c] = cut[first + v][c] + got_pack[number, v, c]
    cut_rows = 3 * pairs_of_groups * ROWS
    replica[pl.ds(0, cut_rows), :] = moved(stacked([value for per in cut for value in per]), spread[...])

    def pack_loads(k):
        return block_loads(
            lambda c, g: replica[
                pl.ds((g // 2 * 3 + c) * ROWS, ROWS), pl.ds((2 * k + g % 2) * LANES, LANES)
            ],
            k,
        )

    from_wall = [near_sums(k, pack_loads(k)) for k in range(cells)]
    for copy in later:
        copy.wait_recv()
    for k in range(cells):
        found = to_cell(k, pair_sums(1, k) + from_wall[k])
        for c in range(3):
            cell_out[k, c] = state[1, k, c] + velocity[k][c] + found[c]

    for copy in edge:
        copy.wait_recv()
    found = stencil(wall_ext1)
    for c in range(3):
        wall_out[c] = wall_ext0[c, centre_rows, centre_lanes] + found[c]
    for copy in spills[1]:
        copy.wait_recv()
    add_spill(1, wall_out)

    for copy in beside + band + spills[0] + packs + later + spills[1] + edge:
        copy.wait_send()


def local(
    n_cell, n_wall,
    self_matrix, cell_source, cell_pos, wall_source, wall_coef, pair_target, pair_source, pair_count, near_wall,
):
    cells, _, _, points = cell_pos.shape
    _, span_theta, span_axial = wall_source.shape
    unknowns = self_matrix.shape[-1]
    wall_tiles = BLOCK * BLOCK // LANES
    tiles = wall_tiles + 2 * cells * (points // LANES)
    rows = -(-tiles // ROWS) * ROWS
    ext_rows = span_theta + 2 * REACH
    ext_lanes = span_axial + 2 * LANES
    vmem = lambda *shape: pltpu.VMEM(shape, F32)
    ints = lambda *shape: pltpu.VMEM(shape, jnp.int32)
    dma = lambda *shape: pltpu.SemaphoreType.DMA(shape)
    hbm = pl.BlockSpec(memory_space=pl.ANY)
    full = pl.BlockSpec(memory_space=pltpu.VMEM)
    by_component = (cells, 3, 1, points)
    velocity, wall = pl.pallas_call(
        functools.partial(body, n_cell, n_wall),
        out_shape=(
            pltpu.VMEM(by_component, F32),
            pltpu.VMEM(wall_source.shape, F32),
        ),
        in_specs=[hbm] * 9,
        out_specs=(full, full),
        scratch_shapes=[
            pltpu.VMEM((cells, unknowns, unknowns), BF16),
            vmem(2, *by_component),
            vmem(2, 2, *by_component),
            vmem(*by_component),
            vmem(2, *by_component),
            vmem(span_theta, span_axial),
            vmem(3, ext_rows, ext_lanes),
            vmem(3, ext_rows, ext_lanes),
            vmem(4, 4, ROWS, LANES),
            vmem(4, 3, ROWS, LANES),
            vmem(8, 2, 4, ROWS, LANES),
            vmem(8, 2, 3, ROWS, LANES),
            vmem(9, 2, 3, ROWS, LANES),
            vmem(8, 2, 3, ROWS, LANES),
            ints(cells, 1, LANES),
            ints(*pair_target.shape),
            ints(*pair_source.shape),
            ints(*pair_count.shape),
            pltpu.VMEM((cells, points, LANES), BF16),
            pltpu.VMEM((cells, BLOCK, tiles * LANES), BF16),
            vmem(cells, 3, rows, LANES),
            pltpu.VMEM((cells, 2 * points, tiles * LANES), BF16),
            vmem(rows * BLOCK, LANES),
            vmem(rows * KINDS, LANES),
            pltpu.VMEM((2 * KINDS, tiles * LANES), BF16),
            pltpu.VMEM((2 * KINDS, 2 * points), BF16),
            vmem(cells, wall_tiles * KINDS, LANES),
            pltpu.VMEM((LANES, 4 * LANES), BF16),
            pltpu.VMEM((4 * LANES, LANES), BF16),
            pltpu.VMEM((LANES, LANES), BF16),
            pltpu.VMEM((cells, LANES, LANES), BF16),
            pltpu.VMEM((cells, LANES, 4 * LANES), BF16),
            vmem(12 * 3 * ROWS, 4 * LANES),
            vmem(3 * ext_rows, LANES),
            dma(8 + cells),
            dma(2),
            dma(2),
            dma(2),
            dma(2),
            dma(8),
            dma(8),
            dma(4),
            dma(4),
            dma(8),
            dma(8),
            dma(2, 8),
            dma(2, 8),
        ],
        compiler_params=pltpu.CompilerParams(
            collective_id=0, has_side_effects=True, vmem_limit_bytes=60 * 2**20
        ),
        cost_estimate=pl.CostEstimate(flops=2 * 10**9, bytes_accessed=8 * 10**6, transcendentals=2 * 10**6),
        name="picard",
    )(
        near_wall, pair_target, pair_source, pair_count,
        self_matrix, cell_source.transpose(0, 2, 1, 3), cell_pos.transpose(0, 2, 1, 3), wall_source, wall_coef,
    )
    return velocity.transpose(0, 2, 1, 3), wall


def solution(mesh):
    placed = (
        P("cell", "wall", None, None),
        P("cell", "wall", None, None),
        P("cell", "wall", None, None),
        P(None, "cell", "wall"),
        P("cell", "wall"),
        P("wall", None),
        P("wall", None),
        P("wall", None),
        P("cell", "wall", None),
    )
    return jax.shard_map(
        functools.partial(local, mesh.shape["cell"], mesh.shape["wall"]),
        mesh=mesh,
        in_specs=placed,
        out_specs=(P("cell", "wall", None, None), P(None, "cell", "wall")),
        check_vma=False,
    )
```

```python
import functools
import math

import jax
import jax.numpy as jnp
from jax import lax
from jax.experimental import pallas as pl
from jax.experimental.pallas import tpu as pltpu
from jax.sharding import PartitionSpec as P

REACH = 16
PAIR_CAP = 8
LANES = 128
ROWS = 8
BLOCK = 2 * REACH
KINDS = 16

panel_step = 0.125
smooth_eps2 = 0.25
panel_weight = 0.015625

MESH = pl.DeviceIdType.MESH
MINOR = (((1,), (1,)), ((), ()))
PLAIN = (((1,), (0,)), ((), ()))

AROUND = ((-1, 0), (1, 0), (0, -1), (0, 1), (-1, -1), (-1, 1), (1, -1), (1, 1))
F32 = jnp.float32
BF16 = jnp.bfloat16


def span(step, low, mid, high):
    return low if step < 0 else (high if step > 0 else mid)


def halves(value):
    high = value.astype(BF16)
    return high, (value - high.astype(F32)).astype(BF16)


def source_kinds(place, load):
    along = place[0] * load[0] + place[1] * load[1] + place[2] * load[2]
    norm = place[0] * place[0] + place[1] * place[1] + place[2] * place[2]
    kinds = [load[0], load[1], load[2]]
    for c in range(3):
        for i in range(3):
            kinds.append(2.0 * load[c] * place[i] + load[i] * place[c])
    for c in range(3):
        kinds.append(along * place[c] + norm * load[c])
    return kinds


def target_sum(place, sums):
    norm = place[0] * place[0] + place[1] * place[1] + place[2] * place[2]
    along = place[0] * sums[0] + place[1] * sums[1] + place[2] * sums[2]
    trace = (sums[3] + sums[7] + sums[11]) * (1.0 / 3.0)
    out = []
    for c in range(3):
        cross = place[0] * sums[3 + 3 * c] + place[1] * sums[4 + 3 * c] + place[2] * sums[5 + 3 * c]
        out.append(
            (norm + 2.0 * smooth_eps2) * sums[c] + place[c] * (along - trace) - cross + sums[12 + c]
        )
    return out


def three(value):
    high = value.astype(BF16).astype(F32)
    rest = value - high
    mid = rest.astype(BF16).astype(F32)
    return high, mid, rest - mid


def square_sides(place, of_target):
    norm = place[0] * place[0] + place[1] * place[1] + place[2] * place[2]
    one = jnp.ones_like(norm)
    rows = []
    for c in range(3):
        high, mid, low = three(place[c] if of_target else -2.0 * place[c])
        rows += [high, high, mid, high, low, mid] if of_target else [high, mid, high, low, high, mid]
    if of_target:
        return rows + [*three(norm + smooth_eps2), one, one, one]
    return rows + [one, one, one, *three(norm)]


def body(
    n_cell,
    n_wall,
    near_hbm,
    target_hbm,
    source_hbm,
    count_hbm,
    matrix_hbm,
    cell_hbm,
    pos_hbm,
    wall_hbm,
    coef_hbm,
    cell_out,
    wall_out,
    matrix,
    state,
    near_state,
    dens1,
    near_dens1,
    coef,
    wall_ext0,
    wall_ext1,
    spill0,
    spill1,
    got_spill0,
    got_spill1,
    pack,
    got_pack,
    own_edge,
    got_edge,
    own_corner,
    got_corner,
    near_own,
    target_row,
    source_row,
    count_row,
    columns,
    sources,
    places,
    level,
    square_f32,
    kinds_f32,
    kinds,
    flat_kinds,
    wall_sums,
    spread,
    gather,
    every,
    unturn,
    turn_spread,
    replica,
    held_groups,
    local_sem,
    state_send,
    state_recv,
    dens_send,
    dens_recv,
    wall_send,
    wall_recv,
    edge_send,
    edge_recv,
    corner_send,
    corner_recv,
    pack_send,
    pack_recv,
    spill_send,
    spill_recv,
):
    cells, points = matrix.shape[0], state.shape[-1]
    span_theta, span_axial = coef.shape
    ext_axial = span_axial + 2 * REACH
    theta_total = span_theta * n_cell
    point_tiles = points // LANES
    wall_tiles = BLOCK * BLOCK // LANES
    tiles = wall_tiles + 2 * cells * point_tiles
    tile_rows = places.shape[2]
    pair_scale = 8.0 / points
    own_tiles = span_axial // LANES
    ext_tiles = own_tiles + 2
    ext_groups = (span_theta + 2 * REACH) // ROWS
    row_groups = span_theta // ROWS + 1
    chunks = BLOCK // ROWS
    pairs_of_groups = ext_groups // 2
    spill, got_spill = (spill0, spill1), (got_spill0, got_spill1)
    me_cell = lax.axis_index("cell")
    me_wall = lax.axis_index("wall")

    def device(step):
        return (
            lax.rem(me_cell + step[0] + n_cell, n_cell),
            lax.rem(me_wall + step[1] + n_wall, n_wall),
        )

    barrier = pltpu.get_barrier_semaphore()
    for step in AROUND:
        pl.semaphore_signal(barrier, inc=1, device_id=device(step), device_id_type=MESH)

    own_near = near_hbm.at[:, :, pl.ds(0, LANES)]
    inside = []
    for number, (src, dst) in enumerate(
        [
            (pos_hbm, state.at[0]),
            (cell_hbm, state.at[1]),
            (own_near, near_own),
            (wall_hbm, wall_ext0.at[:, pl.ds(REACH, span_theta), pl.ds(LANES, span_axial)]),
            (coef_hbm, coef),
            (target_hbm, target_row),
            (source_hbm, source_row),
            (count_hbm, count_row),
        ]
        + [(matrix_hbm.at[k, 0], matrix.at[k]) for k in range(cells)]
    ):
        copy = pltpu.make_async_copy(src, dst, local_sem.at[number])
        copy.start()
        inside.append(copy)

    def remote(src, dst, send, recv, step):
        copy = pltpu.make_async_remote_copy(
            src_ref=src, dst_ref=dst, send_sem=send, recv_sem=recv,
            device_id=device(step), device_id_type=MESH,
        )
        copy.start()
        return copy

    lane_iota = lax.broadcasted_iota(jnp.int32, (ROWS, LANES), 1)
    row_iota = lax.broadcasted_iota(jnp.int32, (ROWS, LANES), 0)
    chunk_iota = lane_iota // BLOCK
    in_block = lane_iota % BLOCK
    block_row = row_iota + ROWS * chunk_iota
    nothing = jnp.zeros((ROWS, LANES), F32)

    in_chunk = lane_iota % BLOCK

    class Block:
        def __init__(self, first):
            first = jnp.broadcast_to(first, (ROWS, LANES))
            self.row = ((first.astype(F32) + 0.5) * (1.0 / ext_axial)).astype(jnp.int32)
            self.column = first.astype(jnp.int32) - self.row * ext_axial
            lane = self.column + (LANES - REACH)
            self.turn = lane & (BLOCK - 1)
            self.shift = self.row & (ROWS - 1)
            self.group = self.row >> 3
            self.where = (lane >> 5) + jnp.where(in_chunk < self.turn, 1, 0) - chunk_iota

    def turn_rows(value, amount):
        for bit in range(3):
            value = jnp.where((amount & (1 << bit)) != 0, pltpu.roll(value, 1 << bit, axis=0), value)
        return value

    def moved(values, matrix_, dims=PLAIN):
        count = values.shape[0]
        terms = jnp.concatenate(three(values), axis=0).astype(BF16)
        out = lax.dot_general(terms, matrix_, dims, preferred_element_type=F32)
        return out[:count] + out[count : 2 * count] + out[2 * count :]

    def stacked(values):
        return jnp.concatenate(values, axis=0)

    def zero_one(mask):
        return jnp.where(mask, 1.0, 0.0).astype(BF16)

    from_lane = lax.broadcasted_iota(jnp.int32, (LANES, LANES), 0)
    to_lane_ = lax.broadcasted_iota(jnp.int32, (LANES, LANES), 1)
    same = (from_lane & (BLOCK - 1)) == (to_lane_ & (BLOCK - 1))
    every[...] = zero_one(same)
    for q in range(chunks):
        spread[:, pl.ds(q * LANES, LANES)] = zero_one(same & (from_lane >> 5 == q))
        gather[pl.ds(q * LANES, LANES), :] = zero_one(same & (to_lane_ >> 5 == q))

    square_f32[...] = jnp.zeros(square_f32.shape, F32)
    kinds_f32[...] = jnp.zeros(kinds_f32.shape, F32)

    inside[0].wait()
    inside[1].wait()
    inside[2].wait()
    own_block = [Block(near_own[k, :, 0:1]) for k in range(cells)]
    width = LANES // cells
    own_first = nothing
    for k in range(cells):
        own_first = jnp.where(lane_iota // width == k, near_own[k, :, 0:1].astype(F32), own_first)
    for k in range(cells):
        turn = jnp.broadcast_to(own_block[k].turn[0:1], (LANES, LANES))
        same = ((from_lane + turn) & (BLOCK - 1)) == (to_lane_ & (BLOCK - 1))
        unturn[k] = zero_one(same & (from_lane >> 5 == to_lane_ >> 5))
        for q in range(chunks):
            turn_spread[k, :, pl.ds(q * LANES, LANES)] = zero_one(same & (from_lane >> 5 == q))

    def rows_of(ref, k):
        return [ref[k, c] for c in range(3)]

    def fill_sources(k, first, count):
        place = [places[k, c, pl.ds(first, count), :] for c in range(3)]
        for n, value in enumerate(square_sides(place, False)):
            square_f32[pl.ds(first * BLOCK + n, count, stride=BLOCK), :] = value
        for a in range(first, min(first + count, tiles)):
            sources[k, :, pl.ds(a * LANES, LANES)] = square_f32[
                pl.ds(a * BLOCK, BLOCK), :
            ].astype(BF16)

    def fill_level(k, first, last):
        def one(step, carry):
            lanes = pl.ds(pl.multiple_of(step * 2 * LANES, 2 * LANES), 2 * LANES)
            square = lax.dot_general(columns[k, :, pl.ds(0, BLOCK)], sources[k, :, lanes], PLAIN, preferred_element_type=F32)
            inverse = lax.rsqrt(square)
            high, low = halves(inverse * inverse * inverse)
            level[k, pl.ds(0, points), lanes] = high
            level[k, pl.ds(points, points), lanes] = low
            return carry

        lax.fori_loop(first // 2, last // 2, one, 0, unroll=True)

    centre, centred = [], []
    for k in range(cells):
        own = rows_of(state.at[0], k)
        mid = [jnp.sum(own[c], axis=1, keepdims=True) * (1.0 / points) for c in range(3)]
        rel = [own[c] - mid[c] for c in range(3)]
        centre.append(mid)
        centred.append(rel)
        rows = square_sides(rel, True)
        rows = jnp.concatenate(rows + [jnp.zeros((LANES - len(rows), points), F32)], axis=0)
        for j in range(point_tiles):
            columns[k, pl.ds(j * LANES, LANES), :] = rows[:, j * LANES : (j + 1) * LANES].T.astype(BF16)
        theta = (me_cell * span_theta - REACH + own_block[k].row + block_row).astype(F32)
        axial = (me_wall * span_axial - REACH + own_block[k].column + in_block).astype(F32)
        angle = (2.0 * math.pi / theta_total) * theta
        radius = theta_total * panel_step / (2.0 * math.pi)
        places[k, 0, pl.ds(0, ROWS), :] = radius * jnp.cos(angle) - mid[0]
        places[k, 1, pl.ds(0, ROWS), :] = radius * jnp.sin(angle) - mid[1]
        places[k, 2, pl.ds(0, ROWS), :] = panel_step * axial - mid[2]
        for c in range(3):
            places[k, c, pl.ds(tiles, tile_rows - tiles), :] = jnp.zeros((tile_rows - tiles, LANES), F32)
        fill_sources(k, 0, wall_tiles)
        fill_level(k, 0, wall_tiles)

    def to_wall(turn):
        merged = [[nothing] * 3 for _ in range(pairs_of_groups)]
        for k in range(cells):
            load = rows_of(state.at[1] if turn == 0 else dens1, k)
            rows = source_kinds(centred[k], [value * pair_scale for value in load])
            rows.append(jnp.zeros_like(rows[0]))
            high, low = halves(jnp.concatenate(rows, axis=0))
            flat_kinds[pl.ds(0, KINDS), pl.ds(0, points)] = high
            flat_kinds[pl.ds(0, KINDS), pl.ds(points, points)] = high
            flat_kinds[pl.ds(KINDS, KINDS), pl.ds(0, points)] = low
            flat_kinds[pl.ds(KINDS, KINDS), pl.ds(points, points)] = low
            sums = lax.dot_general(
                flat_kinds[...], level[k, :, pl.ds(0, wall_tiles * LANES)], PLAIN,
                preferred_element_type=F32,
            )
            sums = sums[:KINDS] + sums[KINDS:]
            for a in range(wall_tiles):
                wall_sums[k, pl.ds(a * KINDS, KINDS), :] = sums[:, a * LANES : (a + 1) * LANES]
            by_kind = [wall_sums[k, pl.ds(n, wall_tiles, stride=KINDS), :] for n in range(15)]
            found = target_sum([places[k, c, pl.ds(0, ROWS), :] for c in range(3)], by_kind)
            block = own_block[k]
            parts = moved(stacked([turn_rows(value, block.shift) for value in found]), turn_spread[k])
            for c in range(3):
                part = [
                    parts[c * ROWS : (c + 1) * ROWS, q * LANES : (q + 1) * LANES] for q in range(chunks)
                ]
                steps = [
                    jnp.where(
                        row_iota >= block.shift,
                        part[j] if j < chunks else nothing,
                        part[j - 1] if j else nothing,
                    )
                    for j in range(chunks + 1)
                ]
                for g in range(ext_groups):
                    value = nothing
                    for r in range(row_groups):
                        if 0 <= g - r <= chunks:
                            value = jnp.where(block.group == r, steps[g - r], value)
                    merged[g // 2][c] = jnp.where(chunk_iota == 2 * k + g % 2, value, merged[g // 2][c])
        for v in range(pairs_of_groups):
            for c in range(3):
                spill[turn][v, c] = merged[v][c]
            if turn == 0:
                spill[turn][v, 3] = own_first

    def cut_of(step):
        return span(step[0], (0, 1), (1, 2), (3, 1))

    def send_spill(turn):
        out = []
        for number, step in enumerate(AROUND):
            first, count = cut_of(step)
            out.append(
                remote(
                    spill[turn].at[pl.ds(first, count)],
                    got_spill[turn].at[number, pl.ds(0, count)],
                    spill_send.at[turn, number],
                    spill_recv.at[turn, number],
                    step,
                )
            )
        return out

    to_wall(0)
    own_rows = pl.ds(REACH, span_theta)
    own_lanes = pl.ds(LANES, span_axial)

    def stage_edge(turn, ref):
        for c in range(3):
            own_edge[turn, 0, c] = ref[c, pl.ds(REACH, 1), own_lanes]
            own_edge[turn, 1, c] = ref[c, pl.ds(REACH + span_theta - 1, 1), own_lanes]

    def send_edge(turn):
        return [
            remote(
                own_edge.at[turn, number], got_edge.at[turn, number],
                edge_send.at[turn, number], edge_recv.at[turn, number], AROUND[number],
            )
            for number in range(2)
        ]

    corner_parts = [(g, c) for g in range(2) for c in range(3)]
    inside[3].wait()
    stage_edge(0, wall_ext0)
    for number, step in enumerate(AROUND[4:]):
        start = span(step[1], 0, 0, LANES - REACH)
        tile = span(step[1], 1, 1, own_tiles)
        value = nothing
        for i, (g, c) in enumerate(corner_parts):
            row = REACH + span(step[0], 0, 0, span_theta - REACH) + ROWS * g
            part = wall_ext0[c, pl.ds(row, ROWS), pl.ds(tile * LANES, LANES)]
            amount = (REACH * i - start) % LANES
            part = pltpu.roll(part, amount, axis=1) if amount else part
            value = jnp.where(lane_iota // REACH == i, part, value)
        own_corner[number] = value
    pl.semaphore_wait(barrier, len(AROUND))

    beside = [
        remote(state, near_state.at[side], state_send.at[side], state_recv.at[side], step)
        for side, step in enumerate(((1, 0), (-1, 0)))
    ]
    edges = [send_edge(0), None]
    spills = [send_spill(0), None]
    corners = [
        remote(
            own_corner.at[number], got_corner.at[number],
            corner_send.at[number], corner_recv.at[number], step,
        )
        for number, step in enumerate(AROUND[4:])
    ]
    band = []
    for number, step in enumerate(AROUND[:4]):
        rows = span(step[0], REACH, span_theta, REACH)
        lanes = span(step[1], LANES, span_axial, LANES)
        from_row = span(step[0], 0, 0, span_theta - REACH)
        from_lane = span(step[1], 0, 0, span_axial - LANES)
        to_row = span(step[0], REACH + span_theta, REACH, 0)
        to_lane = span(step[1], LANES + span_axial, LANES, 0)
        band.append(
            remote(
                wall_hbm.at[:, pl.ds(from_row, rows), pl.ds(from_lane, lanes)],
                wall_ext0.at[:, pl.ds(to_row, rows), pl.ds(to_lane, lanes)],
                wall_send.at[number],
                wall_recv.at[number],
                step,
            )
        )

    def self_term(turn, k):
        flat = jnp.concatenate(rows_of(state.at[1] if turn == 0 else dens1, k), axis=1)
        rows = jnp.broadcast_to(flat, (16, flat.shape[1])).astype(BF16)
        found = lax.dot_general(rows, matrix[k], MINOR, preferred_element_type=F32)
        return [found[0:1, c * points : (c + 1) * points] for c in range(3)]

    for copy in inside[4:]:
        copy.wait()
    velocity = [self_term(0, k) for k in range(cells)]

    slots = target_row.shape[1]
    slot = lax.broadcasted_iota(jnp.int32, (1, slots), 1)
    device_lane = lax.broadcasted_iota(jnp.int32, count_row.shape, 1)
    live = jnp.sum(jnp.where(device_lane == me_cell, count_row[...], 0).astype(F32), axis=1, keepdims=True)
    first_slot = me_cell * PAIR_CAP
    in_use = (slot >= first_slot) & ((slot - first_slot).astype(F32) < live)
    sides = (lax.rem(me_cell + n_cell - 1, n_cell), lax.rem(me_cell + 1, n_cell))
    weight = []
    for k in range(cells):
        mine = in_use & (target_row[...] == me_cell * cells + k)
        weight.append(
            [
                jnp.sum(
                    jnp.where(mine & (source_row[...] == sides[s // cells] * cells + s % cells), pair_scale, 0.0),
                    axis=1,
                    keepdims=True,
                )
                for s in range(2 * cells)
            ]
        )

    for copy in beside:
        copy.wait_recv()
    for k in range(cells):
        for s in range(2 * cells):
            for c in range(3):
                rel = near_state[s // cells, 0, s % cells, c] - centre[k][c]
                for j in range(point_tiles):
                    places[k, c, pl.ds(wall_tiles + s * point_tiles + j, 1), :] = rel[
                        :, j * LANES : (j + 1) * LANES
                    ]
        fill_sources(k, wall_tiles, tile_rows - wall_tiles)
        fill_level(k, wall_tiles, tiles)

    def add_spill(turn, view):
        for half in range(2):
            origins = [(spill[turn], 1 + half, own_where, 0)]
            for number, step in enumerate(AROUND):
                if step[0] == 0:
                    origins.append((got_spill[turn].at[number], half, got_where[number], step[1]))
                elif (step[0] > 0) == (half == 0):
                    origins.append((got_spill[turn].at[number], 0, got_where[number], step[1]))
            replica[pl.ds(0, len(origins) * 3 * ROWS), :] = moved(
                stacked([ref[v, c] for ref, v, _, _ in origins for c in range(3)]), spread[...]
            )
            for t in range(own_tiles):
                sums = {}
                for o, (_, _, blocks, aside) in enumerate(origins):
                    if aside and t != (0 if aside > 0 else own_tiles - 1):
                        continue
                    for k in range(cells):
                        mask = blocks[k] == chunks * (t + 1 + own_tiles * aside)
                        for c in range(3):
                            for g in range(2):
                                part = replica[
                                    pl.ds((3 * o + c) * ROWS, ROWS), pl.ds((2 * k + g) * LANES, LANES)
                                ]
                                part = jnp.where(mask, part, 0.0)
                                sums[c, g] = sums[c, g] + part if (c, g) in sums else part
                for (c, g), value in sums.items():
                    spot = view.at[c, pl.ds(2 * ROWS * half + ROWS * g, ROWS), pl.ds(t * LANES, LANES)]
                    spot[...] = spot[...] + value

    def stencil(ref, turn):
        found = []
        rows = lax.broadcasted_iota(jnp.int32, (span_theta, span_axial), 0)
        for c in range(3):
            wide = ref[c, own_rows, :]
            width_ = wide.shape[1]
            sides_ = pltpu.roll(wide, 1, axis=1) + pltpu.roll(wide, width_ - 1, axis=1)
            mid = ref[c, own_rows, own_lanes]
            up = jnp.where(rows == span_theta - 1, got_edge[turn, 0, c], pltpu.roll(mid, span_theta - 1, axis=0))
            down = jnp.where(rows == 0, got_edge[turn, 1, c], pltpu.roll(mid, 1, axis=0))
            found.append(coef[...] * 0.25 * (up + down + sides_[:, LANES : LANES + span_axial]))
        return found

    def block_loads(groups, k):
        block = own_block[k]
        out = []
        for c in range(3):
            steps = []
            for j in range(chunks + 1):
                value = groups(c, j)
                for r in range(1, row_groups):
                    if j + r < ext_groups:
                        value = jnp.where(block.group == r, groups(c, j + r), value)
                steps.append(turn_rows(value, ROWS - block.shift))
            packed = nothing
            for b in range(chunks):
                part = jnp.where(row_iota + block.shift < ROWS, steps[b], steps[b + 1])
                packed = jnp.where(chunk_iota == b, part, packed)
            out.append(packed)
        out = moved(stacked(out), unturn[k], MINOR)
        return [out[c * ROWS : (c + 1) * ROWS] for c in range(3)]

    def cell_sums(k, first, last, loads):
        count = loads[0].shape[0]
        held = source_kinds([places[k, c, pl.ds(first, count), :] for c in range(3)], loads)
        for n in range(15):
            kinds_f32[pl.ds(first * KINDS + n, count, stride=KINDS), :] = held[n]
        for a in range(first, last):
            high, low = halves(kinds_f32[pl.ds(a * KINDS, KINDS), :])
            kinds[pl.ds(0, KINDS), pl.ds(a * LANES, LANES)] = high
            kinds[pl.ds(KINDS, KINDS), pl.ds(a * LANES, LANES)] = low
        lanes = pl.ds(first * LANES, (last - first) * LANES)
        sums = lax.dot_general(kinds[:, lanes], level[k, :, lanes], MINOR, preferred_element_type=F32)
        sums = sums[:KINDS] + sums[KINDS:]
        return sums[:, :points] + sums[:, points:]

    def pair_sums(turn, k):
        loads = []
        for c in range(3):
            rest = []
            for s in range(2 * cells):
                if turn == 0:
                    beside_load = near_state[s // cells, 1, s % cells, c]
                else:
                    beside_load = near_dens1[s // cells, s % cells, c]
                beside_load = beside_load * weight[k][s]
                for j in range(point_tiles):
                    rest.append(beside_load[:, j * LANES : (j + 1) * LANES])
            rest += [jnp.zeros((1, LANES), F32)] * (tile_rows - tiles)
            loads.append(jnp.concatenate(rest, axis=0))
        return cell_sums(k, wall_tiles, tiles, loads)

    def near_sums(k, picked):
        return cell_sums(k, 0, wall_tiles, [value * panel_weight for value in picked])

    def to_cell(k, sums):
        return target_sum(centred[k], [sums[n : n + 1] for n in range(15)])

    from_pairs = [pair_sums(0, k) for k in range(cells)]

    first_wall = wall_ext1.at[:, own_rows, own_lanes]
    for c in range(3):
        first_wall[c] = wall_ext0[c, own_rows, own_lanes]
    for copy in spills[0]:
        copy.wait_recv()
    got_where = [
        [Block(got_spill0[number, 0, 3, 0:1, k * width : k * width + 1]).where for k in range(cells)]
        for number in range(len(AROUND))
    ]
    own_where = [own_block[k].where for k in range(cells)]
    add_spill(0, first_wall)
    for copy in edges[0] + band[2:]:
        copy.wait_recv()
    found = stencil(wall_ext0, 0)
    for c in range(3):
        first_wall[c] = first_wall[c] + found[c]
    stage_edge(1, wall_ext1)

    units = [(number, v, first) for number, step in enumerate(AROUND)
             for v, first in enumerate(span(step[0], (0,), (0, 2), (2,)))]
    own_units = [(None, 0, 0), (None, 1, 2)]

    def make_packs(units, base):
        for u, (number, v, first) in enumerate(units):
            step = (0, 0) if number is None else AROUND[number]
            blocks = own_where if number is None else got_where[AROUND.index((-step[0], -step[1]))]
            held = span(step[1], [0], range(own_tiles), [own_tiles - 1])
            for k in range(cells):
                masks = [(t, blocks[k] == chunks * (t + 1 - own_tiles * step[1])) for t in held]
                for c in range(3):
                    for g in range(2):
                        rows = pl.ds(REACH + ROWS * (first + g), ROWS)
                        one = nothing
                        for t, mask in masks:
                            one = jnp.where(mask, wall_ext1[c, rows, pl.ds((t + 1) * LANES, LANES)], one)
                        replica[pl.ds(base + (3 * u + c) * ROWS, ROWS), pl.ds((2 * k + g) * LANES, LANES)] = one
        packed = moved(replica[pl.ds(base, 3 * ROWS * len(units)), :], gather[...])
        for u, (number, v, first) in enumerate(units):
            for c in range(3):
                spot = len(AROUND) if number is None else number
                pack[spot, v, c] = packed[(3 * u + c) * ROWS : (3 * u + c + 1) * ROWS]

    make_packs(units, 0)
    packs = []
    for number, step in enumerate(AROUND):
        count = 2 if step[0] == 0 else 1
        packs.append(
            remote(
                pack.at[number, pl.ds(0, count)],
                got_pack.at[number, pl.ds(0, count)],
                pack_send.at[number],
                pack_recv.at[number],
                step,
            )
        )

    def band_loads(k):
        masks = [own_where[k] == chunks * t for t in range(ext_tiles)]
        for c in range(3):
            for g in range(ext_groups):
                value = nothing
                for t in range(ext_tiles):
                    piece = wall_ext0[c, pl.ds(ROWS * g, ROWS), pl.ds(t * LANES, LANES)]
                    value = jnp.where(masks[t], piece, value)
                held_groups[pl.ds((c * ext_groups + g) * ROWS, ROWS), :] = value
        held_groups[...] = moved(held_groups[...], every[...])
        return block_loads(lambda c, g: held_groups[pl.ds((c * ext_groups + g) * ROWS, ROWS), :], k)

    for copy in band[:2] + corners:
        copy.wait_recv()
    for number, step in enumerate(AROUND[4:]):
        start = span(step[1], 0, 0, LANES - REACH)
        tile = span(step[1], ext_tiles - 1, 0, 0)
        for i, (g, c) in enumerate(corner_parts):
            row = span(step[0], REACH + span_theta, 0, 0) + ROWS * g
            amount = (start - REACH * i) % LANES
            part = got_corner[number]
            part = pltpu.roll(part, amount, axis=1) if amount else part
            wall_ext0[c, pl.ds(row, ROWS), pl.ds(tile * LANES, LANES)] = part
    for k in range(cells):
        found = to_cell(k, from_pairs[k] + near_sums(k, band_loads(k)))
        for c in range(3):
            dens1[k, c] = state[1, k, c] + velocity[k][c] + found[c]

    later = [
        remote(dens1, near_dens1.at[side], dens_send.at[side], dens_recv.at[side], step)
        for side, step in enumerate(((1, 0), (-1, 0)))
    ]
    to_wall(1)
    spills[1] = send_spill(1)

    edges[1] = send_edge(1)
    for number, step in enumerate(AROUND[2:4]):
        from_lane = LANES + span(step[1], 0, 0, span_axial - LANES)
        to_lane = span(step[1], LANES + span_axial, LANES, 0)
        edges[1].append(
            remote(
                wall_ext1.at[:, own_rows, pl.ds(from_lane, LANES)],
                wall_ext1.at[:, own_rows, pl.ds(to_lane, LANES)],
                edge_send.at[1, 2 + number],
                edge_recv.at[1, 2 + number],
                step,
            )
        )

    make_packs(own_units, 3 * ROWS * len(units))
    velocity = [self_term(1, k) for k in range(cells)]

    for copy in packs:
        copy.wait_recv()
    cut = [[nothing] * 3 for _ in range(pairs_of_groups)]
    for v in range(2):
        for c in range(3):
            cut[1 + v][c] = pack[len(AROUND), v, c]
    for number, step in enumerate(AROUND):
        first, count = span(step[0], (3, 1), (1, 2), (0, 1))
        for v in range(count):
            for c in range(3):
                cut[first + v][c] = cut[first + v][c] + got_pack[number, v, c]
    cut_rows = 3 * pairs_of_groups * ROWS
    replica[pl.ds(0, cut_rows), :] = moved(stacked([value for per in cut for value in per]), spread[...])

    def pack_loads(k):
        return block_loads(
            lambda c, g: replica[
                pl.ds((g // 2 * 3 + c) * ROWS, ROWS), pl.ds((2 * k + g % 2) * LANES, LANES)
            ],
            k,
        )

    from_wall = [near_sums(k, pack_loads(k)) for k in range(cells)]
    for copy in later:
        copy.wait_recv()
    for k in range(cells):
        found = to_cell(k, pair_sums(1, k) + from_wall[k])
        for c in range(3):
            cell_out[k, c] = state[1, k, c] + velocity[k][c] + found[c]

    for copy in edges[1]:
        copy.wait_recv()
    found = stencil(wall_ext1, 1)
    for c in range(3):
        wall_out[c] = wall_ext0[c, own_rows, own_lanes] + found[c]
    for copy in spills[1]:
        copy.wait_recv()
    add_spill(1, wall_out)

    for copy in beside + band + spills[0] + packs + later + spills[1] + edges[0] + edges[1] + corners:
        copy.wait_send()


def local(
    n_cell, n_wall,
    self_matrix, cell_source, cell_pos, wall_source, wall_coef, pair_target, pair_source, pair_count, near_wall,
):
    cells, _, _, points = cell_pos.shape
    _, span_theta, span_axial = wall_source.shape
    unknowns = self_matrix.shape[-1]
    wall_tiles = BLOCK * BLOCK // LANES
    tiles = wall_tiles + 2 * cells * (points // LANES)
    rows = -(-tiles // ROWS) * ROWS
    ext_rows = span_theta + 2 * REACH
    ext_lanes = span_axial + 2 * LANES
    vmem = lambda *shape: pltpu.VMEM(shape, F32)
    ints = lambda *shape: pltpu.VMEM(shape, jnp.int32)
    dma = lambda *shape: pltpu.SemaphoreType.DMA(shape)
    hbm = pl.BlockSpec(memory_space=pl.ANY)
    full = pl.BlockSpec(memory_space=pltpu.VMEM)
    by_component = (cells, 3, 1, points)
    velocity, wall = pl.pallas_call(
        functools.partial(body, n_cell, n_wall),
        out_shape=(
            pltpu.VMEM(by_component, F32),
            pltpu.VMEM(wall_source.shape, F32),
        ),
        in_specs=[hbm] * 9,
        out_specs=(full, full),
        scratch_shapes=[
            pltpu.VMEM((cells, unknowns, unknowns), BF16),
            vmem(2, *by_component),
            vmem(2, 2, *by_component),
            vmem(*by_component),
            vmem(2, *by_component),
            vmem(span_theta, span_axial),
            vmem(3, ext_rows, ext_lanes),
            vmem(3, ext_rows, ext_lanes),
            vmem(4, 4, ROWS, LANES),
            vmem(4, 3, ROWS, LANES),
            vmem(8, 2, 4, ROWS, LANES),
            vmem(8, 2, 3, ROWS, LANES),
            vmem(9, 2, 3, ROWS, LANES),
            vmem(8, 2, 3, ROWS, LANES),
            vmem(2, 2, 3, 1, span_axial),
            vmem(2, 2, 3, 1, span_axial),
            vmem(4, ROWS, LANES),
            vmem(4, ROWS, LANES),
            ints(cells, 1, LANES),
            ints(*pair_target.shape),
            ints(*pair_source.shape),
            ints(*pair_count.shape),
            pltpu.VMEM((cells, points, LANES), BF16),
            pltpu.VMEM((cells, BLOCK, tiles * LANES), BF16),
            vmem(cells, 3, rows, LANES),
            pltpu.VMEM((cells, 2 * points, tiles * LANES), BF16),
            vmem(rows * BLOCK, LANES),
            vmem(rows * KINDS, LANES),
            pltpu.VMEM((2 * KINDS, tiles * LANES), BF16),
            pltpu.VMEM((2 * KINDS, 2 * points), BF16),
            vmem(cells, wall_tiles * KINDS, LANES),
            pltpu.VMEM((LANES, 4 * LANES), BF16),
            pltpu.VMEM((4 * LANES, LANES), BF16),
            pltpu.VMEM((LANES, LANES), BF16),
            pltpu.VMEM((cells, LANES, LANES), BF16),
            pltpu.VMEM((cells, LANES, 4 * LANES), BF16),
            vmem(12 * 3 * ROWS, 4 * LANES),
            vmem(3 * ext_rows, LANES),
            dma(8 + cells),
            dma(2),
            dma(2),
            dma(2),
            dma(2),
            dma(4),
            dma(4),
            dma(2, 4),
            dma(2, 4),
            dma(4),
            dma(4),
            dma(8),
            dma(8),
            dma(2, 8),
            dma(2, 8),
        ],
        compiler_params=pltpu.CompilerParams(
            collective_id=0, has_side_effects=True, vmem_limit_bytes=60 * 2**20
        ),
        cost_estimate=pl.CostEstimate(flops=2 * 10**9, bytes_accessed=8 * 10**6, transcendentals=2 * 10**6),
        name="picard",
    )(
        near_wall, pair_target, pair_source, pair_count,
        self_matrix, cell_source.transpose(0, 2, 1, 3), cell_pos.transpose(0, 2, 1, 3), wall_source, wall_coef,
    )
    return velocity.transpose(0, 2, 1, 3), wall


def solution(mesh):
    placed = (
        P("cell", "wall", None, None),
        P("cell", "wall", None, None),
        P("cell", "wall", None, None),
        P(None, "cell", "wall"),
        P("cell", "wall"),
        P("wall", None),
        P("wall", None),
        P("wall", None),
        P("cell", "wall", None),
    )
    return jax.shard_map(
        functools.partial(local, mesh.shape["cell"], mesh.shape["wall"]),
        mesh=mesh,
        in_specs=placed,
        out_specs=(P("cell", "wall", None, None), P(None, "cell", "wall")),
        check_vma=False,
    )
```

```python
import functools
import math

import jax
import jax.numpy as jnp
from jax import lax
from jax.experimental import pallas as pl
from jax.experimental.pallas import tpu as pltpu
from jax.sharding import PartitionSpec as P

REACH = 16
PAIR_CAP = 8
LANES = 128
ROWS = 8
BLOCK = 2 * REACH
KINDS = 16

panel_step = 0.125
smooth_eps2 = 0.25
panel_weight = 0.015625

MESH = pl.DeviceIdType.MESH
MINOR = (((1,), (1,)), ((), ()))
PLAIN = (((1,), (0,)), ((), ()))

AROUND = ((-1, 0), (1, 0), (0, -1), (0, 1), (-1, -1), (-1, 1), (1, -1), (1, 1))
F32 = jnp.float32
BF16 = jnp.bfloat16


def span(step, low, mid, high):
    return low if step < 0 else (high if step > 0 else mid)


def halves(value):
    high = value.astype(BF16)
    return high, (value - high.astype(F32)).astype(BF16)


def source_kinds(place, load):
    along = place[0] * load[0] + place[1] * load[1] + place[2] * load[2]
    norm = place[0] * place[0] + place[1] * place[1] + place[2] * place[2]
    kinds = [load[0], load[1], load[2]]
    for c in range(3):
        for i in range(3):
            kinds.append(2.0 * load[c] * place[i] + load[i] * place[c])
    for c in range(3):
        kinds.append(along * place[c] + norm * load[c])
    return kinds


def target_sum(place, sums):
    norm = place[0] * place[0] + place[1] * place[1] + place[2] * place[2]
    along = place[0] * sums[0] + place[1] * sums[1] + place[2] * sums[2]
    trace = (sums[3] + sums[7] + sums[11]) * (1.0 / 3.0)
    out = []
    for c in range(3):
        cross = place[0] * sums[3 + 3 * c] + place[1] * sums[4 + 3 * c] + place[2] * sums[5 + 3 * c]
        out.append(
            (norm + 2.0 * smooth_eps2) * sums[c] + place[c] * (along - trace) - cross + sums[12 + c]
        )
    return out


def three(value):
    high = value.astype(BF16).astype(F32)
    rest = value - high
    mid = rest.astype(BF16).astype(F32)
    return high, mid, rest - mid


def square_sides(place, of_target):
    norm = place[0] * place[0] + place[1] * place[1] + place[2] * place[2]
    one = jnp.ones_like(norm)
    rows = []
    for c in range(3):
        high, mid, low = three(place[c] if of_target else -2.0 * place[c])
        rows += [high, high, mid, high, low, mid] if of_target else [high, mid, high, low, high, mid]
    if of_target:
        return rows + [*three(norm + smooth_eps2), one, one, one]
    return rows + [one, one, one, *three(norm)]


def body(
    n_cell,
    n_wall,
    near_hbm,
    target_hbm,
    source_hbm,
    count_hbm,
    matrix_hbm,
    cell_hbm,
    pos_hbm,
    wall_hbm,
    coef_hbm,
    cell_out,
    wall_out,
    matrix,
    state,
    near_state,
    dens1,
    near_dens1,
    coef,
    wall_ext0,
    wall_ext1,
    spill0,
    spill1,
    got_spill0,
    got_spill1,
    pack,
    got_pack,
    own_edge,
    got_edge,
    own_corner,
    got_corner,
    near_own,
    target_row,
    source_row,
    count_row,
    columns,
    sources,
    places,
    level,
    square_f32,
    kinds_f32,
    kinds,
    flat_kinds,
    wall_sums,
    spread,
    gather,
    every,
    unturn,
    turn_spread,
    replica,
    held_groups,
    local_sem,
    state_send,
    state_recv,
    dens_send,
    dens_recv,
    wall_send,
    wall_recv,
    edge_send,
    edge_recv,
    corner_send,
    corner_recv,
    pack_send,
    pack_recv,
    spill_send,
    spill_recv,
):
    cells, points = matrix.shape[0], state.shape[-1]
    span_theta, span_axial = coef.shape
    ext_axial = span_axial + 2 * REACH
    theta_total = span_theta * n_cell
    point_tiles = points // LANES
    wall_tiles = BLOCK * BLOCK // LANES
    tiles = wall_tiles + 2 * cells * point_tiles
    tile_rows = places.shape[2]
    pair_scale = 8.0 / points
    own_tiles = span_axial // LANES
    ext_tiles = own_tiles + 2
    ext_groups = (span_theta + 2 * REACH) // ROWS
    row_groups = span_theta // ROWS + 1
    chunks = BLOCK // ROWS
    pairs_of_groups = ext_groups // 2
    spill, got_spill = (spill0, spill1), (got_spill0, got_spill1)
    me_cell = lax.axis_index("cell")
    me_wall = lax.axis_index("wall")

    def device(step):
        return (
            lax.rem(me_cell + step[0] + n_cell, n_cell),
            lax.rem(me_wall + step[1] + n_wall, n_wall),
        )

    barrier = pltpu.get_barrier_semaphore()
    for step in AROUND:
        pl.semaphore_signal(barrier, inc=1, device_id=device(step), device_id_type=MESH)

    own_near = near_hbm.at[:, :, pl.ds(0, LANES)]
    inside = []
    for number, (src, dst) in enumerate(
        [
            (pos_hbm, state.at[0]),
            (cell_hbm, state.at[1]),
            (own_near, near_own),
            (wall_hbm, wall_ext0.at[:, pl.ds(REACH, span_theta), pl.ds(LANES, span_axial)]),
            (coef_hbm, coef),
            (target_hbm, target_row),
            (source_hbm, source_row),
            (count_hbm, count_row),
        ]
        + [(matrix_hbm.at[k, 0], matrix.at[k]) for k in range(cells)]
    ):
        copy = pltpu.make_async_copy(src, dst, local_sem.at[number])
        copy.start()
        inside.append(copy)

    def remote(src, dst, send, recv, step):
        copy = pltpu.make_async_remote_copy(
            src_ref=src, dst_ref=dst, send_sem=send, recv_sem=recv,
            device_id=device(step), device_id_type=MESH,
        )
        copy.start()
        return copy

    lane_iota = lax.broadcasted_iota(jnp.int32, (ROWS, LANES), 1)
    row_iota = lax.broadcasted_iota(jnp.int32, (ROWS, LANES), 0)
    chunk_iota = lane_iota // BLOCK
    in_block = lane_iota % BLOCK
    block_row = row_iota + ROWS * chunk_iota
    nothing = jnp.zeros((ROWS, LANES), F32)

    in_chunk = lane_iota % BLOCK

    class Block:
        def __init__(self, first):
            first = jnp.broadcast_to(first, (ROWS, LANES))
            self.row = ((first.astype(F32) + 0.5) * (1.0 / ext_axial)).astype(jnp.int32)
            self.column = first.astype(jnp.int32) - self.row * ext_axial
            lane = self.column + (LANES - REACH)
            self.turn = lane & (BLOCK - 1)
            self.shift = self.row & (ROWS - 1)
            self.group = self.row >> 3
            self.where = (lane >> 5) + jnp.where(in_chunk < self.turn, 1, 0) - chunk_iota

    def turn_rows(value, amount):
        for bit in range(3):
            value = jnp.where((amount & (1 << bit)) != 0, pltpu.roll(value, 1 << bit, axis=0), value)
        return value

    def moved(values, matrix_, dims=PLAIN):
        count = values.shape[0]
        terms = jnp.concatenate(three(values), axis=0).astype(BF16)
        out = lax.dot_general(terms, matrix_, dims, preferred_element_type=F32)
        return out[:count] + out[count : 2 * count] + out[2 * count :]

    def stacked(values):
        return jnp.concatenate(values, axis=0)

    def zero_one(mask):
        return jnp.where(mask, 1.0, 0.0).astype(BF16)

    from_lane = lax.broadcasted_iota(jnp.int32, (LANES, LANES), 0)
    to_lane_ = lax.broadcasted_iota(jnp.int32, (LANES, LANES), 1)
    same = (from_lane & (BLOCK - 1)) == (to_lane_ & (BLOCK - 1))
    every[...] = zero_one(same)
    for q in range(chunks):
        spread[:, pl.ds(q * LANES, LANES)] = zero_one(same & (from_lane >> 5 == q))
        gather[pl.ds(q * LANES, LANES), :] = zero_one(same & (to_lane_ >> 5 == q))

    square_f32[...] = jnp.zeros(square_f32.shape, F32)
    kinds_f32[...] = jnp.zeros(kinds_f32.shape, F32)

    inside[0].wait()
    inside[1].wait()
    inside[2].wait()
    own_block = [Block(near_own[k, :, 0:1]) for k in range(cells)]
    width = LANES // cells
    own_first = nothing
    for k in range(cells):
        own_first = jnp.where(lane_iota // width == k, near_own[k, :, 0:1].astype(F32), own_first)
    for k in range(cells):
        turn = jnp.broadcast_to(own_block[k].turn[0:1], (LANES, LANES))
        same = ((from_lane + turn) & (BLOCK - 1)) == (to_lane_ & (BLOCK - 1))
        unturn[k] = zero_one(same & (from_lane >> 5 == to_lane_ >> 5))
        for q in range(chunks):
            turn_spread[k, :, pl.ds(q * LANES, LANES)] = zero_one(same & (from_lane >> 5 == q))

    def rows_of(ref, k):
        return [ref[k, c] for c in range(3)]

    def fill_sources(k, first, count):
        place = [places[k, c, pl.ds(first, count), :] for c in range(3)]
        for n, value in enumerate(square_sides(place, False)):
            square_f32[pl.ds(first * BLOCK + n, count, stride=BLOCK), :] = value
        for a in range(first, min(first + count, tiles)):
            sources[k, :, pl.ds(a * LANES, LANES)] = square_f32[
                pl.ds(a * BLOCK, BLOCK), :
            ].astype(BF16)

    def fill_level(k, first, last):
        def one(step, carry):
            lanes = pl.ds(pl.multiple_of(step * 2 * LANES, 2 * LANES), 2 * LANES)
            square = lax.dot_general(columns[k, :, pl.ds(0, BLOCK)], sources[k, :, lanes], PLAIN, preferred_element_type=F32)
            inverse = lax.rsqrt(square)
            high, low = halves(inverse * inverse * inverse)
            level[k, pl.ds(0, points), lanes] = high
            level[k, pl.ds(points, points), lanes] = low
            return carry

        lax.fori_loop(first // 2, last // 2, one, 0, unroll=True)

    centre, centred = [], []
    for k in range(cells):
        own = rows_of(state.at[0], k)
        mid = [jnp.sum(own[c], axis=1, keepdims=True) * (1.0 / points) for c in range(3)]
        rel = [own[c] - mid[c] for c in range(3)]
        centre.append(mid)
        centred.append(rel)
        rows = square_sides(rel, True)
        rows = jnp.concatenate(rows + [jnp.zeros((LANES - len(rows), points), F32)], axis=0)
        for j in range(point_tiles):
            columns[k, pl.ds(j * LANES, LANES), :] = rows[:, j * LANES : (j + 1) * LANES].T.astype(BF16)
        theta = (me_cell * span_theta - REACH + own_block[k].row + block_row).astype(F32)
        axial = (me_wall * span_axial - REACH + own_block[k].column + in_block).astype(F32)
        angle = (2.0 * math.pi / theta_total) * theta
        radius = theta_total * panel_step / (2.0 * math.pi)
        places[k, 0, pl.ds(0, ROWS), :] = radius * jnp.cos(angle) - mid[0]
        places[k, 1, pl.ds(0, ROWS), :] = radius * jnp.sin(angle) - mid[1]
        places[k, 2, pl.ds(0, ROWS), :] = panel_step * axial - mid[2]
        for c in range(3):
            places[k, c, pl.ds(tiles, tile_rows - tiles), :] = jnp.zeros((tile_rows - tiles, LANES), F32)
        fill_sources(k, 0, wall_tiles)
        fill_level(k, 0, wall_tiles)

    def to_wall(turn):
        merged = [[nothing] * 3 for _ in range(pairs_of_groups)]
        for k in range(cells):
            load = rows_of(state.at[1] if turn == 0 else dens1, k)
            rows = source_kinds(centred[k], [value * pair_scale for value in load])
            rows.append(jnp.zeros_like(rows[0]))
            high, low = halves(jnp.concatenate(rows, axis=0))
            flat_kinds[pl.ds(0, KINDS), pl.ds(0, points)] = high
            flat_kinds[pl.ds(0, KINDS), pl.ds(points, points)] = high
            flat_kinds[pl.ds(KINDS, KINDS), pl.ds(0, points)] = low
            flat_kinds[pl.ds(KINDS, KINDS), pl.ds(points, points)] = low
            sums = lax.dot_general(
                flat_kinds[...], level[k, :, pl.ds(0, wall_tiles * LANES)], PLAIN,
                preferred_element_type=F32,
            )
            sums = sums[:KINDS] + sums[KINDS:]
            for a in range(wall_tiles):
                wall_sums[k, pl.ds(a * KINDS, KINDS), :] = sums[:, a * LANES : (a + 1) * LANES]
            by_kind = [wall_sums[k, pl.ds(n, wall_tiles, stride=KINDS), :] for n in range(15)]
            found = target_sum([places[k, c, pl.ds(0, ROWS), :] for c in range(3)], by_kind)
            block = own_block[k]
            parts = moved(stacked([turn_rows(value, block.shift) for value in found]), turn_spread[k])
            for c in range(3):
                part = [
                    parts[c * ROWS : (c + 1) * ROWS, q * LANES : (q + 1) * LANES] for q in range(chunks)
                ]
                steps = [
                    jnp.where(
                        row_iota >= block.shift,
                        part[j] if j < chunks else nothing,
                        part[j - 1] if j else nothing,
                    )
                    for j in range(chunks + 1)
                ]
                for g in range(ext_groups):
                    value = nothing
                    for r in range(row_groups):
                        if 0 <= g - r <= chunks:
                            value = jnp.where(block.group == r, steps[g - r], value)
                    merged[g // 2][c] = jnp.where(chunk_iota == 2 * k + g % 2, value, merged[g // 2][c])
        for v in range(pairs_of_groups):
            for c in range(3):
                spill[turn][v, c] = merged[v][c]
            if turn == 0:
                spill[turn][v, 3] = own_first

    def cut_of(step):
        return span(step[0], (0, 1), (1, 2), (3, 1))

    def send_spill(turn):
        out = []
        for number, step in enumerate(AROUND):
            first, count = cut_of(step)
            out.append(
                remote(
                    spill[turn].at[pl.ds(first, count)],
                    got_spill[turn].at[number, pl.ds(0, count)],
                    spill_send.at[turn, number],
                    spill_recv.at[turn, number],
                    step,
                )
            )
        return out

    to_wall(0)
    own_rows = pl.ds(REACH, span_theta)
    own_lanes = pl.ds(LANES, span_axial)

    def stage_edge(turn, ref):
        for c in range(3):
            own_edge[turn, 0, c] = ref[c, pl.ds(REACH, 1), own_lanes]
            own_edge[turn, 1, c] = ref[c, pl.ds(REACH + span_theta - 1, 1), own_lanes]

    def send_edge(turn):
        return [
            remote(
                own_edge.at[turn, number], got_edge.at[turn, number],
                edge_send.at[turn, number], edge_recv.at[turn, number], AROUND[number],
            )
            for number in range(2)
        ]

    corner_parts = [(g, c) for g in range(2) for c in range(3)]
    inside[3].wait()
    stage_edge(0, wall_ext0)
    for number, step in enumerate(AROUND[4:]):
        start = span(step[1], 0, 0, LANES - REACH)
        tile = span(step[1], 1, 1, own_tiles)
        value = nothing
        for i, (g, c) in enumerate(corner_parts):
            row = REACH + span(step[0], 0, 0, span_theta - REACH) + ROWS * g
            part = wall_ext0[c, pl.ds(row, ROWS), pl.ds(tile * LANES, LANES)]
            amount = (REACH * i - start) % LANES
            part = pltpu.roll(part, amount, axis=1) if amount else part
            value = jnp.where(lane_iota // REACH == i, part, value)
        own_corner[number] = value
    pl.semaphore_wait(barrier, len(AROUND))

    beside = [
        remote(state, near_state.at[side], state_send.at[side], state_recv.at[side], step)
        for side, step in enumerate(((1, 0), (-1, 0)))
    ]
    edges = [send_edge(0), None]
    spills = [send_spill(0), None]
    corners = [
        remote(
            own_corner.at[number], got_corner.at[number],
            corner_send.at[number], corner_recv.at[number], step,
        )
        for number, step in enumerate(AROUND[4:])
    ]
    band = []
    for number, step in enumerate(AROUND[:4]):
        rows = span(step[0], REACH, span_theta, REACH)
        lanes = span(step[1], LANES, span_axial, LANES)
        from_row = span(step[0], 0, 0, span_theta - REACH)
        from_lane = span(step[1], 0, 0, span_axial - LANES)
        to_row = span(step[0], REACH + span_theta, REACH, 0)
        to_lane = span(step[1], LANES + span_axial, LANES, 0)
        band.append(
            remote(
                wall_hbm.at[:, pl.ds(from_row, rows), pl.ds(from_lane, lanes)],
                wall_ext0.at[:, pl.ds(to_row, rows), pl.ds(to_lane, lanes)],
                wall_send.at[number],
                wall_recv.at[number],
                step,
            )
        )

    def self_terms(turn):
        ref = state.at[1] if turn == 0 else dens1
        size = matrix.shape[1]
        half = LANES
        whole = size - half
        upper = lax.broadcasted_iota(jnp.int32, (16, size), 0) < ROWS
        flat = [jnp.concatenate(rows_of(ref, k), axis=1) for k in range(cells)]
        both = jnp.where(upper, flat[0], flat[1])
        split = jnp.concatenate(
            [jnp.where(upper[:, :half], both[:, whole:], 0.0), jnp.where(upper[:, :half], 0.0, both[:, whole:])],
            axis=1,
        ).astype(BF16)
        front = both[:, :whole].astype(BF16)
        tail = jnp.concatenate([matrix[k, :, pl.ds(whole, half)] for k in range(cells)], axis=1)
        last = jnp.concatenate([matrix[k, pl.ds(whole, half), pl.ds(0, whole)] for k in range(cells)], axis=0)
        tail = lax.dot_general(split, tail, MINOR, preferred_element_type=F32)
        last = lax.dot_general(front, last, MINOR, preferred_element_type=F32)
        out = []
        for k in range(cells):
            main = lax.dot_general(
                front, matrix[k, pl.ds(0, whole), pl.ds(0, whole)], MINOR, preferred_element_type=F32
            )
            row = ROWS * k
            found = jnp.concatenate(
                [main[row : row + 1], last[row : row + 1, half * k : half * (k + 1)]], axis=1
            ) + tail[row : row + 1]
            out.append([found[:, c * points : (c + 1) * points] for c in range(3)])
        return out

    for copy in inside[4:]:
        copy.wait()
    velocity = self_terms(0)

    slots = target_row.shape[1]
    slot = lax.broadcasted_iota(jnp.int32, (1, slots), 1)
    device_lane = lax.broadcasted_iota(jnp.int32, count_row.shape, 1)
    live = jnp.sum(jnp.where(device_lane == me_cell, count_row[...], 0).astype(F32), axis=1, keepdims=True)
    first_slot = me_cell * PAIR_CAP
    in_use = (slot >= first_slot) & ((slot - first_slot).astype(F32) < live)
    sides = (lax.rem(me_cell + n_cell - 1, n_cell), lax.rem(me_cell + 1, n_cell))
    weight = []
    for k in range(cells):
        mine = in_use & (target_row[...] == me_cell * cells + k)
        weight.append(
            [
                jnp.sum(
                    jnp.where(mine & (source_row[...] == sides[s // cells] * cells + s % cells), pair_scale, 0.0),
                    axis=1,
                    keepdims=True,
                )
                for s in range(2 * cells)
            ]
        )

    for copy in beside:
        copy.wait_recv()
    for k in range(cells):
        for s in range(2 * cells):
            for c in range(3):
                rel = near_state[s // cells, 0, s % cells, c] - centre[k][c]
                for j in range(point_tiles):
                    places[k, c, pl.ds(wall_tiles + s * point_tiles + j, 1), :] = rel[
                        :, j * LANES : (j + 1) * LANES
                    ]
        fill_sources(k, wall_tiles, tile_rows - wall_tiles)
        fill_level(k, wall_tiles, tiles)

    def add_spill(turn, view):
        for half in range(2):
            origins = [(spill[turn], 1 + half, own_where, 0)]
            for number, step in enumerate(AROUND):
                if step[0] == 0:
                    origins.append((got_spill[turn].at[number], half, got_where[number], step[1]))
                elif (step[0] > 0) == (half == 0):
                    origins.append((got_spill[turn].at[number], 0, got_where[number], step[1]))
            replica[pl.ds(0, len(origins) * 3 * ROWS), :] = moved(
                stacked([ref[v, c] for ref, v, _, _ in origins for c in range(3)]), spread[...]
            )
            for t in range(own_tiles):
                sums = {}
                for o, (_, _, blocks, aside) in enumerate(origins):
                    if aside and t != (0 if aside > 0 else own_tiles - 1):
                        continue
                    for k in range(cells):
                        mask = blocks[k] == chunks * (t + 1 + own_tiles * aside)
                        for c in range(3):
                            for g in range(2):
                                part = replica[
                                    pl.ds((3 * o + c) * ROWS, ROWS), pl.ds((2 * k + g) * LANES, LANES)
                                ]
                                part = jnp.where(mask, part, 0.0)
                                sums[c, g] = sums[c, g] + part if (c, g) in sums else part
                for (c, g), value in sums.items():
                    spot = view.at[c, pl.ds(2 * ROWS * half + ROWS * g, ROWS), pl.ds(t * LANES, LANES)]
                    spot[...] = spot[...] + value

    def stencil(ref, turn):
        found = []
        rows = lax.broadcasted_iota(jnp.int32, (span_theta, span_axial), 0)
        for c in range(3):
            wide = ref[c, own_rows, :]
            width_ = wide.shape[1]
            sides_ = pltpu.roll(wide, 1, axis=1) + pltpu.roll(wide, width_ - 1, axis=1)
            mid = ref[c, own_rows, own_lanes]
            up = jnp.where(rows == span_theta - 1, got_edge[turn, 0, c], pltpu.roll(mid, span_theta - 1, axis=0))
            down = jnp.where(rows == 0, got_edge[turn, 1, c], pltpu.roll(mid, 1, axis=0))
            found.append(coef[...] * 0.25 * (up + down + sides_[:, LANES : LANES + span_axial]))
        return found

    def block_loads(groups, k):
        block = own_block[k]
        out = []
        for c in range(3):
            steps = []
            for j in range(chunks + 1):
                value = groups(c, j)
                for r in range(1, row_groups):
                    if j + r < ext_groups:
                        value = jnp.where(block.group == r, groups(c, j + r), value)
                steps.append(turn_rows(value, ROWS - block.shift))
            packed = nothing
            for b in range(chunks):
                part = jnp.where(row_iota + block.shift < ROWS, steps[b], steps[b + 1])
                packed = jnp.where(chunk_iota == b, part, packed)
            out.append(packed)
        out = moved(stacked(out), unturn[k], MINOR)
        return [out[c * ROWS : (c + 1) * ROWS] for c in range(3)]

    def cell_sums(k, first, last, loads):
        count = loads[0].shape[0]
        held = source_kinds([places[k, c, pl.ds(first, count), :] for c in range(3)], loads)
        for n in range(15):
            kinds_f32[pl.ds(first * KINDS + n, count, stride=KINDS), :] = held[n]
        for a in range(first, last):
            high, low = halves(kinds_f32[pl.ds(a * KINDS, KINDS), :])
            kinds[pl.ds(0, KINDS), pl.ds(a * LANES, LANES)] = high
            kinds[pl.ds(KINDS, KINDS), pl.ds(a * LANES, LANES)] = low
        lanes = pl.ds(first * LANES, (last - first) * LANES)
        sums = lax.dot_general(kinds[:, lanes], level[k, :, lanes], MINOR, preferred_element_type=F32)
        sums = sums[:KINDS] + sums[KINDS:]
        return sums[:, :points] + sums[:, points:]

    def pair_sums(turn, k):
        loads = []
        for c in range(3):
            rest = []
            for s in range(2 * cells):
                if turn == 0:
                    beside_load = near_state[s // cells, 1, s % cells, c]
                else:
                    beside_load = near_dens1[s // cells, s % cells, c]
                beside_load = beside_load * weight[k][s]
                for j in range(point_tiles):
                    rest.append(beside_load[:, j * LANES : (j + 1) * LANES])
            rest += [jnp.zeros((1, LANES), F32)] * (tile_rows - tiles)
            loads.append(jnp.concatenate(rest, axis=0))
        return cell_sums(k, wall_tiles, tiles, loads)

    def near_sums(k, picked):
        return cell_sums(k, 0, wall_tiles, [value * panel_weight for value in picked])

    def to_cell(k, sums):
        return target_sum(centred[k], [sums[n : n + 1] for n in range(15)])

    from_pairs = [pair_sums(0, k) for k in range(cells)]

    first_wall = wall_ext1.at[:, own_rows, own_lanes]
    for c in range(3):
        first_wall[c] = wall_ext0[c, own_rows, own_lanes]
    for copy in spills[0]:
        copy.wait_recv()
    got_where = [
        [Block(got_spill0[number, 0, 3, 0:1, k * width : k * width + 1]).where for k in range(cells)]
        for number in range(len(AROUND))
    ]
    own_where = [own_block[k].where for k in range(cells)]
    add_spill(0, first_wall)
    for copy in edges[0] + band[2:]:
        copy.wait_recv()
    found = stencil(wall_ext0, 0)
    for c in range(3):
        first_wall[c] = first_wall[c] + found[c]
    stage_edge(1, wall_ext1)

    units = [(number, v, first) for number, step in enumerate(AROUND)
             for v, first in enumerate(span(step[0], (0,), (0, 2), (2,)))]
    own_units = [(None, 0, 0), (None, 1, 2)]

    def make_packs(units, base):
        for u, (number, v, first) in enumerate(units):
            step = (0, 0) if number is None else AROUND[number]
            blocks = own_where if number is None else got_where[AROUND.index((-step[0], -step[1]))]
            held = span(step[1], [0], range(own_tiles), [own_tiles - 1])
            for k in range(cells):
                masks = [(t, blocks[k] == chunks * (t + 1 - own_tiles * step[1])) for t in held]
                for c in range(3):
                    for g in range(2):
                        rows = pl.ds(REACH + ROWS * (first + g), ROWS)
                        one = nothing
                        for t, mask in masks:
                            one = jnp.where(mask, wall_ext1[c, rows, pl.ds((t + 1) * LANES, LANES)], one)
                        replica[pl.ds(base + (3 * u + c) * ROWS, ROWS), pl.ds((2 * k + g) * LANES, LANES)] = one
        packed = moved(replica[pl.ds(base, 3 * ROWS * len(units)), :], gather[...])
        for u, (number, v, first) in enumerate(units):
            for c in range(3):
                spot = len(AROUND) if number is None else number
                pack[spot, v, c] = packed[(3 * u + c) * ROWS : (3 * u + c + 1) * ROWS]

    make_packs(units, 0)
    packs = []
    for number, step in enumerate(AROUND):
        count = 2 if step[0] == 0 else 1
        packs.append(
            remote(
                pack.at[number, pl.ds(0, count)],
                got_pack.at[number, pl.ds(0, count)],
                pack_send.at[number],
                pack_recv.at[number],
                step,
            )
        )

    def band_loads(k):
        masks = [own_where[k] == chunks * t for t in range(ext_tiles)]
        for c in range(3):
            for g in range(ext_groups):
                value = nothing
                for t in range(ext_tiles):
                    piece = wall_ext0[c, pl.ds(ROWS * g, ROWS), pl.ds(t * LANES, LANES)]
                    value = jnp.where(masks[t], piece, value)
                held_groups[pl.ds((c * ext_groups + g) * ROWS, ROWS), :] = value
        held_groups[...] = moved(held_groups[...], every[...])
        return block_loads(lambda c, g: held_groups[pl.ds((c * ext_groups + g) * ROWS, ROWS), :], k)

    for copy in band[:2] + corners:
        copy.wait_recv()
    for number, step in enumerate(AROUND[4:]):
        start = span(step[1], 0, 0, LANES - REACH)
        tile = span(step[1], ext_tiles - 1, 0, 0)
        for i, (g, c) in enumerate(corner_parts):
            row = span(step[0], REACH + span_theta, 0, 0) + ROWS * g
            amount = (start - REACH * i) % LANES
            part = got_corner[number]
            part = pltpu.roll(part, amount, axis=1) if amount else part
            wall_ext0[c, pl.ds(row, ROWS), pl.ds(tile * LANES, LANES)] = part
    for k in range(cells):
        found = to_cell(k, from_pairs[k] + near_sums(k, band_loads(k)))
        for c in range(3):
            dens1[k, c] = state[1, k, c] + velocity[k][c] + found[c]

    later = [
        remote(dens1, near_dens1.at[side], dens_send.at[side], dens_recv.at[side], step)
        for side, step in enumerate(((1, 0), (-1, 0)))
    ]
    to_wall(1)
    spills[1] = send_spill(1)

    edges[1] = send_edge(1)
    for number, step in enumerate(AROUND[2:4]):
        from_lane = LANES + span(step[1], 0, 0, span_axial - LANES)
        to_lane = span(step[1], LANES + span_axial, LANES, 0)
        edges[1].append(
            remote(
                wall_ext1.at[:, own_rows, pl.ds(from_lane, LANES)],
                wall_ext1.at[:, own_rows, pl.ds(to_lane, LANES)],
                edge_send.at[1, 2 + number],
                edge_recv.at[1, 2 + number],
                step,
            )
        )

    make_packs(own_units, 3 * ROWS * len(units))
    velocity = self_terms(1)

    for copy in packs:
        copy.wait_recv()
    cut = [[nothing] * 3 for _ in range(pairs_of_groups)]
    for v in range(2):
        for c in range(3):
            cut[1 + v][c] = pack[len(AROUND), v, c]
    for number, step in enumerate(AROUND):
        first, count = span(step[0], (3, 1), (1, 2), (0, 1))
        for v in range(count):
            for c in range(3):
                cut[first + v][c] = cut[first + v][c] + got_pack[number, v, c]
    cut_rows = 3 * pairs_of_groups * ROWS
    replica[pl.ds(0, cut_rows), :] = moved(stacked([value for per in cut for value in per]), spread[...])

    def pack_loads(k):
        return block_loads(
            lambda c, g: replica[
                pl.ds((g // 2 * 3 + c) * ROWS, ROWS), pl.ds((2 * k + g % 2) * LANES, LANES)
            ],
            k,
        )

    from_wall = [near_sums(k, pack_loads(k)) for k in range(cells)]
    for copy in later:
        copy.wait_recv()
    for k in range(cells):
        found = to_cell(k, pair_sums(1, k) + from_wall[k])
        for c in range(3):
            cell_out[k, c] = state[1, k, c] + velocity[k][c] + found[c]

    for copy in edges[1]:
        copy.wait_recv()
    found = stencil(wall_ext1, 1)
    for c in range(3):
        wall_out[c] = wall_ext0[c, own_rows, own_lanes] + found[c]
    for copy in spills[1]:
        copy.wait_recv()
    add_spill(1, wall_out)

    for copy in beside + band + spills[0] + packs + later + spills[1] + edges[0] + edges[1] + corners:
        copy.wait_send()


def local(
    n_cell, n_wall,
    self_matrix, cell_source, cell_pos, wall_source, wall_coef, pair_target, pair_source, pair_count, near_wall,
):
    cells, _, _, points = cell_pos.shape
    _, span_theta, span_axial = wall_source.shape
    unknowns = self_matrix.shape[-1]
    wall_tiles = BLOCK * BLOCK // LANES
    tiles = wall_tiles + 2 * cells * (points // LANES)
    rows = -(-tiles // ROWS) * ROWS
    ext_rows = span_theta + 2 * REACH
    ext_lanes = span_axial + 2 * LANES
    vmem = lambda *shape: pltpu.VMEM(shape, F32)
    ints = lambda *shape: pltpu.VMEM(shape, jnp.int32)
    dma = lambda *shape: pltpu.SemaphoreType.DMA(shape)
    hbm = pl.BlockSpec(memory_space=pl.ANY)
    full = pl.BlockSpec(memory_space=pltpu.VMEM)
    by_component = (cells, 3, 1, points)
    velocity, wall = pl.pallas_call(
        functools.partial(body, n_cell, n_wall),
        out_shape=(
            pltpu.VMEM(by_component, F32),
            pltpu.VMEM(wall_source.shape, F32),
        ),
        in_specs=[hbm] * 9,
        out_specs=(full, full),
        scratch_shapes=[
            pltpu.VMEM((cells, unknowns, unknowns), BF16),
            vmem(2, *by_component),
            vmem(2, 2, *by_component),
            vmem(*by_component),
            vmem(2, *by_component),
            vmem(span_theta, span_axial),
            vmem(3, ext_rows, ext_lanes),
            vmem(3, ext_rows, ext_lanes),
            vmem(4, 4, ROWS, LANES),
            vmem(4, 3, ROWS, LANES),
            vmem(8, 2, 4, ROWS, LANES),
            vmem(8, 2, 3, ROWS, LANES),
            vmem(9, 2, 3, ROWS, LANES),
            vmem(8, 2, 3, ROWS, LANES),
            vmem(2, 2, 3, 1, span_axial),
            vmem(2, 2, 3, 1, span_axial),
            vmem(4, ROWS, LANES),
            vmem(4, ROWS, LANES),
            ints(cells, 1, LANES),
            ints(*pair_target.shape),
            ints(*pair_source.shape),
            ints(*pair_count.shape),
            pltpu.VMEM((cells, points, LANES), BF16),
            pltpu.VMEM((cells, BLOCK, tiles * LANES), BF16),
            vmem(cells, 3, rows, LANES),
            pltpu.VMEM((cells, 2 * points, tiles * LANES), BF16),
            vmem(rows * BLOCK, LANES),
            vmem(rows * KINDS, LANES),
            pltpu.VMEM((2 * KINDS, tiles * LANES), BF16),
            pltpu.VMEM((2 * KINDS, 2 * points), BF16),
            vmem(cells, wall_tiles * KINDS, LANES),
            pltpu.VMEM((LANES, 4 * LANES), BF16),
            pltpu.VMEM((4 * LANES, LANES), BF16),
            pltpu.VMEM((LANES, LANES), BF16),
            pltpu.VMEM((cells, LANES, LANES), BF16),
            pltpu.VMEM((cells, LANES, 4 * LANES), BF16),
            vmem(12 * 3 * ROWS, 4 * LANES),
            vmem(3 * ext_rows, LANES),
            dma(8 + cells),
            dma(2),
            dma(2),
            dma(2),
            dma(2),
            dma(4),
            dma(4),
            dma(2, 4),
            dma(2, 4),
            dma(4),
            dma(4),
            dma(8),
            dma(8),
            dma(2, 8),
            dma(2, 8),
        ],
        compiler_params=pltpu.CompilerParams(
            collective_id=0, has_side_effects=True, vmem_limit_bytes=60 * 2**20
        ),
        cost_estimate=pl.CostEstimate(flops=2 * 10**9, bytes_accessed=8 * 10**6, transcendentals=2 * 10**6),
        name="picard",
    )(
        near_wall, pair_target, pair_source, pair_count,
        self_matrix, cell_source.transpose(0, 2, 1, 3), cell_pos.transpose(0, 2, 1, 3), wall_source, wall_coef,
    )
    return velocity.transpose(0, 2, 1, 3), wall


def solution(mesh):
    placed = (
        P("cell", "wall", None, None),
        P("cell", "wall", None, None),
        P("cell", "wall", None, None),
        P(None, "cell", "wall"),
        P("cell", "wall"),
        P("wall", None),
        P("wall", None),
        P("wall", None),
        P("cell", "wall", None),
    )
    return jax.shard_map(
        functools.partial(local, mesh.shape["cell"], mesh.shape["wall"]),
        mesh=mesh,
        in_specs=placed,
        out_specs=(P("cell", "wall", None, None), P(None, "cell", "wall")),
        check_vma=False,
    )
```
